256 devices in a mesh: dp: 32 (over x, z), tensor: 8 (over y, core).
Axes of the slice: x: 4, y: 4, z: 8, core: 2. Of those that a mesh axis runs over, the one named last changes fastest.
Arguments:
- cache_kv: bfloat16 [256, 2, 1024, 8, 128], P('dp', None, None, 'tensor'), may hold values from -6 to 6
- lengths: int32 [256], replicated, may hold values from 64 to 1024, as said below
- step_kv: bfloat16 [2, 256, 2, 8, 128], P(None, 'dp', None, 'tensor'), as said below
- queries: bfloat16 [2, 256, 64, 128], P(None, 'dp', 'tensor'), as said below
- parents: int32 [256], replicated, may hold values from 0 to 15, as said below
- finished: int32 [256], P('dp'), may hold values from 0 to 1, as said below
- reward_in: bfloat16 [8192, 4096], P('tensor', 'dp'), may hold values from -0.0625 to 0.0625
- reward_head: bfloat16 [4096], P('dp'), may hold values from -0.09375 to 0.09375
Outputs:
- first_out: bfloat16 [256, 8192], P('dp', 'tensor')
- second_out: bfloat16 [256, 8192], P('dp', 'tensor')
- scores: float32 [256], P('dp')
- new_cache: bfloat16 [256, 2, 1024, 8, 128], P('dp', None, None, 'tensor')
The draws below stay inside these ranges and needn't reach their ends.
Inputs may be any that keep to these rules, and one draw needn't show every extreme that they name: `lengths`: multiples of 64; in every draw some beam has all 1024 positions valid. Beams b * 8 to b * 8 + 7 lie on one device; parents name beams of the same problem; on each device at most 4 slots name a parent of the other half of the problem, and in every draw some device has exactly 4. At most 4 finished beams among the 8 of one device; some device has exactly 4 in every draw. `step_kv`: new keys and values of order one. `queries`: queries of order one or larger.
All inputs are finite; a program needn't handle non-finite values.
Results may differ from the reference program's by a relative error of at most 0.0072.
Values may be sent and summed in bfloat16 or wider, within the bound.
No kernel may reach another device: no remote copies, remote signals or barrier semaphores. Data moves between devices by JAX's collectives and lax.ppermute only.
A program may use at most 128 MiB of HBM per device.

```python
import math
import jax
import jax.numpy as jnp
from jax import lax

HEADS = 64
KV_HEADS = 8
HEAD_DIM = 128
D_GEN = 8192
D_RM = 4096
BEAMS = 16
BEAM_DEV = 8
CACHE = 1024
SEND_MOST = 4
FINISH_MOST = 4
TOTAL_BEAMS = 256


def new_tokens(key):
    return jax.random.normal(key, (2, TOTAL_BEAMS, 2, KV_HEADS, HEAD_DIM), jnp.float32)


def draw_step_kv(key, part):
    base = new_tokens(key)
    return base.astype(jnp.bfloat16)


def draw_queries(key, part):
    key = jax.random.fold_in(key, 12)
    first_key = jax.random.fold_in(key, 0)
    values = jax.random.normal(first_key, (2, TOTAL_BEAMS, HEADS, HEAD_DIM), jnp.float32)
    return values.astype(jnp.bfloat16)


def draw_lengths(key, part):
    key = jax.random.fold_in(key, 13)
    first_key, second_key = jax.random.split(key)
    blocks = jax.random.randint(first_key, (TOTAL_BEAMS,), 1, CACHE // 64 + 1)
    chosen = jax.random.randint(second_key, (), 0, TOTAL_BEAMS)
    blocks = jnp.where(jnp.arange(TOTAL_BEAMS) == chosen, CACHE // 64, blocks)
    return (blocks * 64).astype(jnp.int32)


def chosen_slots(key, most):
    groups = TOTAL_BEAMS // BEAM_DEV
    first_key, second_key, third_key = jax.random.split(key, 3)
    counts = jax.random.randint(first_key, (groups,), 0, most + 1)
    chosen = jax.random.randint(second_key, (), 0, groups)
    counts = jnp.where(jnp.arange(groups) == chosen, most, counts)
    ranking = jax.random.randint(third_key, (groups, BEAM_DEV), 0, 1 << 20) * BEAM_DEV + jnp.arange(BEAM_DEV)[None, :]
    order = jnp.argsort(jnp.argsort(ranking, axis=1), axis=1)
    return order < counts[:, None]


def draw_parents(key, part):
    key = jax.random.fold_in(key, 14)
    first_key, second_key = jax.random.split(key)
    groups = TOTAL_BEAMS // BEAM_DEV
    crossing = chosen_slots(first_key, SEND_MOST)
    within = jax.random.randint(second_key, (groups, BEAM_DEV), 0, BEAM_DEV)
    own_half = (jnp.arange(groups) % 2)[:, None]
    picked = within + BEAM_DEV * jnp.where(crossing, 1 - own_half, own_half)
    return picked.reshape(-1).astype(jnp.int32)


def draw_finished(key, part):
    key = jax.random.fold_in(key, 15)
    marked = chosen_slots(key, FINISH_MOST)
    return marked.reshape(-1).astype(jnp.int32)


def steps_of(own_key, extent, pieces, least, top_value):
    level = 1.0
    for dim, shards_of in pieces:
        draws = jax.random.uniform(jax.random.fold_in(jax.random.fold_in(own_key, 6), dim), (shards_of,), jnp.float32, least / len(pieces), top_value / len(pieces))
        level = level * jnp.repeat(jnp.exp(draws), extent[dim] // shards_of).reshape((-1,) + (1,) * (len(extent) - 1 - dim))
    return level


def noise(rng, shape, width, most, shards=(), kind=jnp.bfloat16):
    values = jax.random.normal(rng, shape, jnp.float32) * width
    if len(shards) > 0:
        values = steps_of(rng, shape, shards, -0.22, 0.18) * values
    return jnp.clip(values, min=-most, max=most).astype(kind)


def setup_inputs(seed: int = 0) -> dict:
    seeds = jax.random.split(jax.random.key(seed), 9)
    cache_kv = noise(seeds[0], (TOTAL_BEAMS, 2, CACHE, KV_HEADS, HEAD_DIM), 1.0, 6.0, ((0, 32), (3, 8)))
    lengths = draw_lengths(jax.random.fold_in(seeds[8], 71), 0)
    step_kv = draw_step_kv(jax.random.fold_in(seeds[8], 71), 0)
    queries = draw_queries(jax.random.fold_in(seeds[8], 71), 0)
    parents = draw_parents(jax.random.fold_in(seeds[8], 71), 0)
    finished = draw_finished(jax.random.fold_in(seeds[8], 71), 0)
    reward_in = noise(seeds[6], (D_GEN, D_RM), D_GEN ** -0.5, 0.0625, ((0, 8), (1, 32)))
    reward_head = noise(seeds[7], (D_RM,), D_RM ** -0.5, 0.09375, ((0, 32),))
    return dict(cache_kv=cache_kv, lengths=lengths, step_kv=step_kv, queries=queries, parents=parents, finished=finished, reward_in=reward_in, reward_head=reward_head)


def attend(query_block, key_rows, value_rows, valid_length, extra_keys, extra_values):
    scaling = 1.0 / math.sqrt(query_block.shape[-1])
    query_wide = query_block.astype(jnp.float32)
    logits = jnp.einsum('bgrd,bcgd->bgrc', query_wide, key_rows.astype(jnp.float32)) * scaling
    places = lax.broadcasted_iota(jnp.int32, logits.shape, 3)
    logits = jnp.where(places < valid_length[:, None, None, None], logits, -1e+30)
    extra_logits = jnp.einsum('bgrd,begd->bgre', query_wide, extra_keys.astype(jnp.float32)) * scaling
    peak = jnp.maximum(lax.optimization_barrier(jnp.max(logits, axis=3, keepdims=True)), lax.optimization_barrier(jnp.max(extra_logits, axis=3, keepdims=True)))
    cached = jnp.exp(logits - peak)
    fresh = jnp.exp(extra_logits - peak)
    total = lax.optimization_barrier(jnp.sum(cached, axis=3, keepdims=True)) + lax.optimization_barrier(jnp.sum(fresh, axis=3, keepdims=True))
    weights = (cached / total).astype(jnp.bfloat16).astype(jnp.float32)
    extra_weights = (fresh / total).astype(jnp.bfloat16).astype(jnp.float32)
    mixed = jnp.einsum('bgrc,bcgd->bgrd', weights, value_rows.astype(jnp.float32))
    mixed = mixed + jnp.einsum('bgre,begd->bgrd', extra_weights, extra_values.astype(jnp.float32))
    return mixed.astype(jnp.bfloat16).reshape(mixed.shape[0], -1)

def reference(cache_kv, lengths, step_kv, queries, parents, finished, reward_in, reward_head):
    per_group = HEADS // KV_HEADS

    def one_beam(slot):
        anchor = slot // BEAMS * BEAMS + parents[slot]
        query_one = queries[0, slot].reshape(1, KV_HEADS, per_group, HEAD_DIM)
        query_two = queries[1, slot].reshape(1, KV_HEADS, per_group, HEAD_DIM)
        own_cache = cache_kv[slot]
        first = attend(query_one, own_cache[0][None], own_cache[1][None], lengths[slot][None], step_kv[0, slot, 0][None, None], step_kv[0, slot, 1][None, None])
        parent_cache = cache_kv[anchor]
        extra_keys = jnp.stack([step_kv[0, anchor, 0], step_kv[1, slot, 0]])[None]
        extra_values = jnp.stack([step_kv[0, anchor, 1], step_kv[1, slot, 1]])[None]
        second = attend(query_two, parent_cache[0][None], parent_cache[1][None], lengths[anchor][None], extra_keys, extra_values)
        return (first[0], second[0], parent_cache)
    first_out, second_out, new_cache = lax.map(one_beam, jnp.arange(TOTAL_BEAMS, dtype=jnp.int32))
    rows_wide = second_out.astype(jnp.float32)
    mean_square = lax.optimization_barrier(jnp.mean(rows_wide * rows_wide, axis=1, keepdims=True))
    normed = (rows_wide * lax.rsqrt(mean_square + 1e-05)).astype(jnp.bfloat16)
    hidden = jnp.dot(normed, reward_in, preferred_element_type=jnp.float32)
    totals = lax.optimization_barrier(jnp.sum(jax.nn.silu(hidden) * reward_head.astype(jnp.float32)[None, :], axis=1))
    scores = jnp.where(finished == 1, totals, jnp.zeros_like(totals))
    return (first_out, second_out, scores, new_cache)
```

```python
import functools
import math

import jax
import jax.numpy as jnp
from jax import lax
from jax.experimental import pallas as pl
from jax.experimental.pallas import tpu as pltpu
from jax.sharding import PartitionSpec as P

D_GEN = 8192
MOST = 4
BD = 8
CACHE = 1024
HD = 128
GH = 8
F32 = jnp.float32
BF16 = jnp.bfloat16
VM = pltpu.VMEM
SM = pltpu.SMEM
HB = pltpu.HBM


def spec(space):
    return pl.BlockSpec(memory_space=space)


def needed(par_ref, slots_at, half):
    flags = []
    for b in range(BD):
        want = half * BD + b
        hit = par_ref[slots_at] == want
        for j in range(1, BD):
            hit = hit | (par_ref[slots_at + j] == want)
        flags.append(hit)
    return flags


def pack_kernel(par_ref, cache_ref, w_ref, head_ref, packed_ref, wext_ref, hscr, sems, wsem, hsem):
    me = lax.axis_index("dp")
    half = lax.rem(me, 2)
    start = (me - half) * BD + (1 - half) * BD
    flags = needed(par_ref, start, half)
    rank = jnp.int32(0)
    for b in range(BD):
        slot = jnp.minimum(rank, MOST - 1)

        @pl.when(flags[b] & (rank < MOST))
        def _():
            pltpu.make_async_copy(cache_ref.at[b], packed_ref.at[slot], sems.at[slot]).start()

        rank = rank + flags[b].astype(jnp.int32)
    rows = w_ref.shape[0]
    wcopy = pltpu.make_async_copy(w_ref, wext_ref.at[pl.ds(0, rows)], wsem)
    wcopy.start()
    hscr[...] = jnp.broadcast_to(head_ref[...].astype(F32), (16, HD)).astype(BF16)
    hcopy = pltpu.make_async_copy(hscr, wext_ref.at[pl.ds(rows, 16)], hsem)
    hcopy.start()
    hcopy.wait()
    wcopy.wait()
    for r in range(MOST):

        @pl.when(r < rank)
        def _():
            pltpu.make_async_copy(cache_ref.at[0], packed_ref.at[r], sems.at[r]).wait()


def attend_kernel(
    par_ref, len_ref, fino_ref, finr_ref, cache_ref, qo_ref, qr_ref, kvo_ref, kvr_ref,
    first_ref, own_ref, other_ref, rows_ref, newc_ref,
    buf, q1s, e1s, v1s, pcol, fscr, acc, rscr, pk, insem, outsem,
):
    me = lax.axis_index("dp")
    half = lax.rem(me, 2)
    pair = (me - half) * BD
    mine = pair + half * BD
    theirs = pair + (1 - half) * BD
    scaling = 1.0 / math.sqrt(HD)
    for b in range(BD):
        pltpu.make_async_copy(cache_ref.at[b], buf.at[b], insem.at[b]).start()
    own_local = []
    q1s[...] = jnp.zeros_like(q1s)
    for b in range(BD):
        q1s[b, 0:GH, :] = qo_ref[0, b]
    e1s[...] = jnp.full_like(e1s, -1e30)
    v1s[...] = jnp.zeros_like(v1s)
    for s in range(2 * BD):
        at = (mine if s < BD else theirs) + s % BD
        parent = par_ref[at]
        here = (parent >= half * BD) & (parent < half * BD + BD)
        local = jnp.where(here, parent - half * BD, -1)
        if s < BD:
            own_local.append(local)
        rows = pl.ds(s * GH, GH)
        pcol[rows, :] = jnp.full((GH, HD), local, jnp.int32)
        q = (qo_ref if s < BD else qr_ref)[1, s % BD].astype(F32)
        kv = kvo_ref if s < BD else kvr_ref
        k1 = kv[1, s % BD, 0:1, :].astype(F32)
        e1s[rows, :] = jnp.broadcast_to(jnp.sum(q * k1, axis=1, keepdims=True) * scaling, (GH, HD))
        v1s[rows, :] = jnp.broadcast_to(kv[1, s % BD, 1:2, :].astype(F32), (GH, HD))
    q2 = jnp.concatenate(
        [qo_ref[1].reshape(BD * GH, HD), qr_ref[1].reshape(BD * GH, HD)], axis=0
    )
    acc[...] = jnp.zeros_like(acc)
    for b in range(BD):
        pltpu.make_async_copy(cache_ref.at[b], buf.at[b], insem.at[b]).wait()
        for s in range(BD):

            @pl.when(own_local[s] == b)
            def _():
                pltpu.make_async_copy(buf.at[b], newc_ref.at[s], outsem.at[s]).start()

        length = len_ref[mine + b]
        q = jnp.concatenate([q2, q1s[b]], axis=0)
        logits = lax.dot_general(
            q, buf[b, 0], (((1,), (1,)), ((), ())), preferred_element_type=F32
        ) * scaling
        places = lax.broadcasted_iota(jnp.int32, logits.shape, 1)
        logits = jnp.where(places < length, logits, -1e30)
        k0 = kvo_ref[0, b, 0:1, :].astype(F32)
        v0 = kvo_ref[0, b, 1:2, :].astype(F32)
        e0 = jnp.sum(q.astype(F32) * k0, axis=1, keepdims=True) * scaling
        e1 = e1s[:, 0:1]
        peak = jnp.maximum(jnp.maximum(jnp.max(logits, axis=1, keepdims=True), e0), e1)
        p = jnp.exp(logits - peak)
        p0 = jnp.exp(e0 - peak)
        p1 = jnp.exp(e1 - peak)
        inv = 1.0 / (jnp.sum(p, axis=1, keepdims=True) + p0 + p1)
        mixed = jnp.dot((p * inv).astype(BF16), buf[b, 1], preferred_element_type=F32)
        mixed = mixed + (p0 * inv).astype(BF16).astype(F32) * v0
        mixed = mixed + (p1 * inv).astype(BF16).astype(F32) * v1s[...]
        fscr[b * GH : (b + 1) * GH, :] = mixed[2 * BD * GH : 2 * BD * GH + GH]
        acc[...] = jnp.where(pcol[...] == b, mixed[: 2 * BD * GH], acc[...])
    for h in range(GH):
        lanes = slice(h * HD, (h + 1) * HD)
        first_ref[:, lanes] = fscr[pl.ds(h, BD, stride=GH), :].astype(BF16)
        rscr[0:BD, lanes] = acc[pl.ds(h, BD, stride=GH), :].astype(BF16).astype(F32)
        rscr[BD : 2 * BD, lanes] = acc[pl.ds(BD * GH + h, BD, stride=GH), :].astype(BF16).astype(F32)
    own_ref[...] = rscr[0:BD, :].astype(BF16)
    other_ref[...] = rscr[BD : 2 * BD, :].astype(BF16)
    pk[...] = jnp.zeros_like(pk)
    rank = jnp.int32(0)
    for j in range(2 * BD):
        owned = half == j // BD
        flag = jnp.where(owned, fino_ref[j % BD], finr_ref[j % BD]) == 1
        source = jnp.where(owned, 0, BD) + j % BD

        @pl.when(flag)
        def _():
            pk[pl.ds(jnp.minimum(rank, BD - 1), 1), :] = rscr[pl.ds(source, 1), :]

        rank = rank + flag.astype(jnp.int32)
    packed = pk[...].astype(BF16)
    for k in range(rows_ref.shape[0]):
        rows_ref[k] = packed
    for s in range(BD):

        @pl.when(own_local[s] >= 0)
        def _():
            pltpu.make_async_copy(buf.at[0], newc_ref.at[s], outsem.at[s]).wait()


def place_kernel(par_ref, recv_ref, into_ref, newc_ref, sems):
    del into_ref
    me = lax.axis_index("dp")
    half = lax.rem(me, 2)
    mine = (me - half) * BD + half * BD
    flags = needed(par_ref, mine, 1 - half)
    ranks = []
    rank = jnp.int32(0)
    for b in range(BD):
        ranks.append(rank)
        rank = rank + flags[b].astype(jnp.int32)
    crossing = []
    for s in range(BD):
        parent = par_ref[mine + s]
        local = parent - (1 - half) * BD
        cross = (local >= 0) & (local < BD)
        slot = jnp.int32(0)
        for b in range(BD):
            slot = jnp.where(local == b, ranks[b], slot)
        slot = jnp.minimum(slot, MOST - 1)
        crossing.append(cross)

        @pl.when(cross)
        def _():
            pltpu.make_async_copy(recv_ref.at[slot], newc_ref.at[s], sems.at[s]).start()

    for s in range(BD):

        @pl.when(crossing[s])
        def _():
            pltpu.make_async_copy(recv_ref.at[0], newc_ref.at[s], sems.at[s]).wait()


def hidden_kernel(rows_ref, w0, w1, w2, w3, out_ref):
    depth = w0.shape[0] - 16
    rows = jnp.concatenate(
        [
            rows_ref[2 * p].astype(F32) + rows_ref[2 * p + 1].astype(F32)
            for p in range(rows_ref.shape[0] // 2)
        ],
        axis=0,
    )
    narrow = rows.astype(BF16)
    parts = [
        jnp.dot(narrow, w[0:depth, :], preferred_element_type=F32) for w in (w0, w1, w2, w3)
    ]
    squares = jnp.sum(rows * rows, axis=1, keepdims=True)
    parts.append(jnp.broadcast_to(squares, (rows.shape[0], HD)))
    for k in range(out_ref.shape[0]):
        for i, part in enumerate(parts):
            out_ref[k, :, i * HD : (i + 1) * HD] = part


def score_kernel(hid_ref, w0, w1, w2, w3, out_ref):
    depth = w0.shape[0] - 16
    total = hid_ref[0]
    for k in range(1, hid_ref.shape[0]):
        total = total + hid_ref[k]
    factor = lax.rsqrt(total[:, 4 * HD : 4 * HD + 1] / D_GEN + 1e-05)
    sums = jnp.zeros((total.shape[0], 1), F32)
    for i, w in enumerate((w0, w1, w2, w3)):
        head = w[depth : depth + 16, :].astype(F32)[0:1, :]
        v = total[:, i * HD : (i + 1) * HD] * factor
        sums = sums + jnp.sum(v / (1.0 + jnp.exp(-v)) * head, axis=1, keepdims=True)
    wide = jnp.broadcast_to(sums, (total.shape[0], HD))
    for z in range(out_ref.shape[0]):
        p = z // 2
        out_ref[z] = wide[p * BD : (p + 1) * BD]


def final_kernel(fino_ref, finr_ref, part_ref, out_ref, scr):
    me = lax.axis_index("dp")
    half = lax.rem(me, 2)
    total = part_ref[0]
    for k in range(1, part_ref.shape[0]):
        total = total + part_ref[k]
    scr[...] = total
    rank = jnp.int32(0)
    for j in range(BD):
        rank = rank + jnp.where(half == 1, (finr_ref[j] == 1).astype(jnp.int32), 0)
    for s in range(BD):
        flag = fino_ref[s] == 1
        value = scr[pl.ds(jnp.minimum(rank, BD - 1), 1), :][0, 0]
        out_ref[s] = jnp.where(flag, value, 0.0)
        rank = rank + flag.astype(jnp.int32)


def call(kernel, outs, ins, out_specs, scratch=(), aliases=None, cost=None, limit=None):
    return functools.partial(
        pl.pallas_call,
        kernel,
        out_shape=outs,
        in_specs=[spec(s) for s in ins],
        out_specs=[spec(s) for s in out_specs],
        scratch_shapes=list(scratch),
        input_output_aliases=aliases or {},
        compiler_params=pltpu.CompilerParams(vmem_limit_bytes=limit or 40 * 1024 * 1024),
        cost_estimate=pl.CostEstimate(flops=cost or 1000000, bytes_accessed=cost or 1000000, transcendentals=0),
    )()


def shape(dims, dtype):
    return jax.ShapeDtypeStruct(dims, dtype)


def swap(array):
    return lax.ppermute(array, "dp", [(i, i ^ 1) for i in range(lax.axis_size("dp"))])


def per_device(nx, nz, cache_kv, lengths, step_kv, queries, parents, finished, reward_in, reward_head):
    ndp = nx * nz
    zgroups = [[a * nz + b for b in range(nz)] for a in range(nx)]
    nt = lax.axis_size("tensor")
    cache = cache_kv.reshape(BD, 2, CACHE, HD)
    kv = step_kv.reshape(2, BD, 2, HD)
    depth = reward_in.shape[0]
    recv_q = swap(queries)
    recv_kv = swap(kv)
    recv_fin = swap(finished)
    packed, wext = call(
        pack_kernel,
        [shape((MOST, 2, CACHE, HD), BF16), shape((depth + 16, HD), BF16)],
        [SM, HB, HB, VM],
        [HB, HB],
        [VM((16, HD), BF16), pltpu.SemaphoreType.DMA((MOST,)), pltpu.SemaphoreType.DMA, pltpu.SemaphoreType.DMA],
    )(parents, cache, reward_in, reward_head.reshape(1, HD))
    recv_cache = swap(packed)
    others = [
        lax.ppermute(wext, "dp", [(i, (i + nz * k) % ndp) for i in range(ndp)]) for k in range(1, nx)
    ]
    first_out, own_out, other_out, rows, newc = call(
        attend_kernel,
        [
            shape((BD, GH * HD), BF16),
            shape((BD, GH * HD), BF16),
            shape((BD, GH * HD), BF16),
            shape((nz, BD, GH * HD), BF16),
            shape((BD, 2, CACHE, HD), BF16),
        ],
        [SM, SM, SM, SM, HB, VM, VM, VM, VM],
        [VM, VM, VM, VM, HB],
        [
            VM((BD, 2, CACHE, HD), BF16),
            VM((BD, 2 * GH, HD), BF16),
            VM((2 * BD * GH + 16, HD), F32),
            VM((2 * BD * GH + 16, HD), F32),
            VM((2 * BD * GH, HD), jnp.int32),
            VM((BD * GH, HD), F32),
            VM((2 * BD * GH, HD), F32),
            VM((2 * BD, GH * HD), F32),
            VM((BD, GH * HD), F32),
            pltpu.SemaphoreType.DMA((BD,)),
            pltpu.SemaphoreType.DMA((BD,)),
        ],
        cost=20000000,
    )(parents, lengths, finished, recv_fin, cache, queries, recv_q, kv, recv_kv)
    second_out = own_out + swap(other_out)
    gathered = lax.all_to_all(rows, "dp", 0, 0, axis_index_groups=zgroups, tiled=True)
    (partial,) = call(
        hidden_kernel, [shape((nt, nz // 2 * BD, 5 * HD), F32)], [VM] * 5, [VM]
    )(gathered, wext, *others)
    partials = lax.all_to_all(partial, "tensor", 0, 0, tiled=True)
    (sums,) = call(score_kernel, [shape((nz, BD, HD), F32)], [VM] * 5, [VM])(partials, wext, *others)
    sums = lax.all_to_all(sums, "dp", 0, 0, axis_index_groups=zgroups, tiled=True)
    (scores,) = call(
        final_kernel, [shape((BD,), F32)], [SM, SM, VM], [SM], [VM((BD, HD), F32)]
    )(finished, recv_fin, sums)
    (new_cache,) = call(
        place_kernel,
        [shape((BD, 2, CACHE, HD), BF16)],
        [SM, HB, HB],
        [HB],
        [pltpu.SemaphoreType.DMA((BD,))],
        aliases={2: 0},
    )(parents, recv_cache, newc)
    return (first_out, second_out, scores, new_cache.reshape(cache_kv.shape))


def solution(mesh):
    ndp = mesh.shape["dp"]
    nx = 4
    return jax.shard_map(
        functools.partial(per_device, nx, ndp // nx),
        mesh=mesh,
        in_specs=(
            P("dp", None, None, "tensor", None),
            P(),
            P(None, "dp", None, "tensor", None),
            P(None, "dp", "tensor", None),
            P(),
            P("dp"),
            P("tensor", "dp"),
            P("dp"),
        ),
        out_specs=(
            P("dp", "tensor"),
            P("dp", "tensor"),
            P("dp"),
            P("dp", None, None, "tensor", None),
        ),
        check_vma=False,
    )
```

```python
import functools
import math

import jax
import jax.numpy as jnp
from jax import lax
from jax.experimental import pallas as pl
from jax.experimental.pallas import tpu as pltpu
from jax.sharding import PartitionSpec as P

D_GEN = 8192
MOST = 4
BD = 8
CACHE = 1024
HD = 128
GH = 8
F32 = jnp.float32
BF16 = jnp.bfloat16
VM = pltpu.VMEM
SM = pltpu.SMEM
HB = pltpu.HBM


def spec(space):
    return pl.BlockSpec(memory_space=space)


def needed(par_ref, slots_at, half):
    flags = []
    for b in range(BD):
        want = half * BD + b
        hit = par_ref[slots_at] == want
        for j in range(1, BD):
            hit = hit | (par_ref[slots_at + j] == want)
        flags.append(hit)
    return flags


def ranked(flags):
    ranks = []
    rank = jnp.int32(0)
    for flag in flags:
        ranks.append(rank)
        rank = rank + flag.astype(jnp.int32)
    return ranks, rank


def message_kernel(fin_ref, q_ref, kv_ref, w_ref, head_ref, msg_ref, wext_ref, wsem):
    rows = w_ref.shape[0]
    wcopy = pltpu.make_async_copy(w_ref, wext_ref.at[pl.ds(0, rows)], wsem)
    wcopy.start()
    wext_ref[pl.ds(rows, 16), :] = jnp.broadcast_to(head_ref[...].astype(F32), (16, HD)).astype(BF16)
    for s in range(BD):
        step = kv_ref[1, s].astype(F32)
        flag = jnp.full((1, HD), fin_ref[s], jnp.int32).astype(F32)
        msg_ref[s] = jnp.concatenate(
            [q_ref[1, s].astype(F32), step, flag, jnp.zeros((5, HD), F32)], axis=0
        ).astype(BF16)
    wcopy.wait()


def pack_kernel(par_ref, cache_ref, after_ref, a_ref, sems):
    me = lax.axis_index("dp")
    half = lax.rem(me, 2)
    start = (me - half) * BD + (1 - half) * BD
    flags = needed(par_ref, start, half)
    ranks, total = ranked(flags)
    odd = lax.rem(lax.axis_index("tensor"), 2) == 1
    early = a_ref.shape[0]
    for b in range(BD):
        for r in range(min(b + 1, early)):

            @pl.when(flags[b] & (ranks[b] == r) & odd)
            def _():
                pltpu.make_async_copy(cache_ref.at[b], a_ref.at[r], sems.at[r]).start()

    for r in range(early):

        @pl.when((r < total) & odd)
        def _():
            pltpu.make_async_copy(cache_ref.at[0], a_ref.at[r], sems.at[r]).wait()


OWN = BD * GH
ALL = OWN + MOST * GH
ROWS = ALL + 2 * GH


def attend_kernel(
    par_ref, len_ref, fin_ref, cache_ref, q_ref, kv_ref, msg_ref,
    first_ref, own_ref, swap_ref, rows_ref, meta_ref, even_ref, odd_ref, newc_ref,
    buf, q2s, q1s, e1s, v1s, pcol, fscr, acc, rscr, crow, pk, insem, outsem, sendsem,
):
    me = lax.axis_index("dp")
    half = lax.rem(me, 2)
    pair = (me - half) * BD
    mine = pair + half * BD
    theirs = pair + (1 - half) * BD
    scaling = math.log2(math.e) / math.sqrt(HD)
    for b in range(BD):
        pltpu.make_async_copy(cache_ref.at[b], buf.at[b], insem.at[b]).start()
    q1s[...] = jnp.zeros_like(q1s)
    for b in range(BD):
        q1s[b, 0:GH, :] = q_ref[0, b]
    e1s[...] = jnp.full_like(e1s, -1e30)
    v1s[...] = jnp.zeros_like(v1s)
    own_local = []
    for s in range(BD):
        local = par_ref[mine + s] - half * BD
        local = jnp.where((local >= 0) & (local < BD), local, -1)
        own_local.append(local)
        rows = pl.ds(s * GH, GH)
        pcol[rows, :] = jnp.full((GH, HD), local, jnp.int32)
        q = q_ref[1, s].astype(F32)
        step = kv_ref[1, s].astype(F32)
        q2s[rows, :] = q
        e1s[rows, :] = jnp.broadcast_to(
            jnp.sum(q * step[0:1], axis=1, keepdims=True) * scaling, (GH, HD)
        )
        v1s[rows, :] = jnp.broadcast_to(step[1:2], (GH, HD))
    slots = [jnp.int32(0)] * MOST
    locals_ = [jnp.int32(-1)] * MOST
    count = jnp.int32(0)
    for s in range(BD):
        local = par_ref[theirs + s] - half * BD
        here = (local >= 0) & (local < BD)
        for j in range(min(s + 1, MOST)):
            take = here & (count == j)
            slots[j] = jnp.where(take, s, slots[j])
            locals_[j] = jnp.where(take, local, locals_[j])
        count = count + here.astype(jnp.int32)
    for j in range(MOST):
        rows = pl.ds(OWN + j * GH, GH)
        pcol[rows, :] = jnp.full((GH, HD), locals_[j], jnp.int32)
        block = msg_ref[slots[j]].astype(F32)
        q = block[0:GH]
        q2s[rows, :] = q
        e1s[rows, :] = jnp.broadcast_to(
            jnp.sum(q * block[GH : GH + 1], axis=1, keepdims=True) * scaling, (GH, HD)
        )
        v1s[rows, :] = jnp.broadcast_to(block[GH + 1 : GH + 2], (GH, HD))
    q2 = q2s[...].astype(BF16)
    acc[...] = jnp.zeros_like(acc)
    wanted = needed(par_ref, theirs, half)
    send_ranks, send_total = ranked(wanted)
    skip = MOST - odd_ref.shape[0]
    core = lax.rem(lax.axis_index("tensor"), 2)
    for b in range(BD):
        pltpu.make_async_copy(cache_ref.at[b], buf.at[b], insem.at[b]).wait()
        for r in range(min(b + 1, MOST)):

            @pl.when(wanted[b] & (send_ranks[b] == r) & (core == 0))
            def _():
                pltpu.make_async_copy(buf.at[b], even_ref.at[r], sendsem.at[r]).start()

            if r >= skip:

                @pl.when(wanted[b] & (send_ranks[b] == r) & (core == 1))
                def _():
                    pltpu.make_async_copy(buf.at[b], odd_ref.at[r - skip], sendsem.at[r]).start()

        for s in range(BD):

            @pl.when(own_local[s] == b)
            def _():
                pltpu.make_async_copy(buf.at[b], newc_ref.at[s], outsem.at[s]).start()

        length = len_ref[mine + b]
        q = jnp.concatenate([q2, q1s[b]], axis=0)
        logits = lax.dot_general(
            q, buf[b, 0], (((1,), (1,)), ((), ())), preferred_element_type=F32
        ) * scaling
        places = lax.broadcasted_iota(jnp.int32, logits.shape, 1)
        logits = jnp.where(places < length, logits, -1e30)
        step = kv_ref[0, b].astype(F32)
        e0 = jnp.sum(q.astype(F32) * step[0:1], axis=1, keepdims=True) * scaling
        e1 = e1s[:, 0:1]
        peak = jnp.maximum(jnp.maximum(jnp.max(logits, axis=1, keepdims=True), e0), e1)
        p = jnp.exp2(logits - peak)
        p0 = jnp.exp2(e0 - peak)
        p1 = jnp.exp2(e1 - peak)
        inv = 1.0 / (jnp.sum(p, axis=1, keepdims=True) + p0 + p1)
        mixed = jnp.dot((p * inv).astype(BF16), buf[b, 1], preferred_element_type=F32)
        mixed = mixed + (p0 * inv).astype(BF16).astype(F32) * step[1:2]
        mixed = mixed + (p1 * inv).astype(BF16).astype(F32) * v1s[...]
        fscr[b * GH : (b + 1) * GH, :] = mixed[ALL : ALL + GH]
        acc[...] = jnp.where(pcol[...] == b, mixed[:ALL], acc[...])
    rscr[...] = jnp.zeros_like(rscr)
    for h in range(GH):
        lanes = slice(h * HD, (h + 1) * HD)
        first_ref[:, lanes] = fscr[pl.ds(h, BD, stride=GH), :].astype(BF16)
        rscr[0:BD, lanes] = acc[pl.ds(h, BD, stride=GH), :].astype(BF16).astype(F32)
        crow[0:MOST, lanes] = acc[pl.ds(OWN + h, MOST, stride=GH), :].astype(BF16).astype(F32)
    for j in range(MOST):

        @pl.when(j < count)
        def _():
            rscr[pl.ds(BD + slots[j], 1), :] = crow[j : j + 1, :]

    own_ref[...] = rscr[0:BD, :].astype(BF16)
    pk[...] = jnp.zeros_like(pk)
    rank = jnp.int32(0)
    before = jnp.int32(0)
    for j in range(2 * BD):
        owned = half == j // BD
        theirs_flag = msg_ref[j % BD].astype(F32)[GH + 2 : GH + 3, :][0, 0] > 0.5
        flag = jnp.where(owned, (fin_ref[j % BD] == 1).astype(jnp.int32), theirs_flag.astype(jnp.int32))
        source = jnp.where(owned, 0, BD) + j % BD

        @pl.when(flag == 1)
        def _():
            pk[pl.ds(jnp.minimum(rank, BD - 1), 1), :] = rscr[pl.ds(source, 1), :]

        if j < BD:
            before = before + jnp.where(half == 1, flag, 0)
        rank = rank + flag
    packed = pk[...].astype(BF16)
    rows_ref[...] = packed
    swap_ref[...] = jnp.concatenate([rscr[BD : 2 * BD, :], pk[...]], axis=0).astype(BF16)
    ranks, _ = ranked(needed(par_ref, mine, 1 - half))
    for s in range(BD):
        local = par_ref[mine + s] - (1 - half) * BD
        slot = jnp.int32(-1)
        for b in range(BD):
            slot = jnp.where(local == b, ranks[b], slot)
        meta_ref[s : s + 1, :] = jnp.full((1, HD), slot, jnp.int32)
        flag = (fin_ref[s] == 1).astype(jnp.int32)
        place_at = jnp.where(flag == 1, jnp.minimum(before, BD - 1), -1)
        meta_ref[BD + s : BD + s + 1, :] = jnp.full((1, HD), place_at, jnp.int32)
        before = before + flag
    for r in range(MOST):

        @pl.when((r < send_total) & ((core == 0) | (r >= skip)))
        def _():
            pltpu.make_async_copy(buf.at[0], even_ref.at[0], sendsem.at[r]).wait()

    for s in range(BD):

        @pl.when(own_local[s] >= 0)
        def _():
            pltpu.make_async_copy(buf.at[0], newc_ref.at[s], outsem.at[s]).wait()


def place_start(first, parity, meta_ref, recv_ref, newc_ref, sems):
    crossing = []
    count = recv_ref.shape[0]
    core = lax.rem(lax.axis_index("tensor"), 2)
    for s in range(BD):
        slot = meta_ref[s : s + 1, :][0, 0] - first
        cross = (slot >= 0) & (slot < count) & (core == parity)
        slot = jnp.clip(slot, 0, count - 1)
        crossing.append(cross)

        @pl.when(cross)
        def _():
            pltpu.make_async_copy(recv_ref.at[slot], newc_ref.at[s], sems.at[s]).start()

    return crossing


def place_wait(crossing, recv_ref, newc_ref, sems):
    for s in range(BD):

        @pl.when(crossing[s])
        def _():
            pltpu.make_async_copy(recv_ref.at[0], newc_ref.at[s], sems.at[s]).wait()


def place_kernel(first, parity, meta_ref, recv_ref, *refs):
    newc_ref, sems = refs[-2:]
    waits = place_start(first, parity, meta_ref, recv_ref, newc_ref, sems)
    place_wait(waits, recv_ref, newc_ref, sems)


def gate_kernel(*refs):
    del refs


def join_kernel(parity, own_ref, rows_ref, swap_ref, meta_ref, recv_ref, *refs):
    second_ref, full_ref, _, newc_ref, sems = refs[-5:]
    waits = place_start(0, parity, meta_ref, recv_ref, newc_ref, sems)
    second_ref[...] = own_ref[...] + swap_ref[0:BD, :]
    full_ref[...] = rows_ref[...] + swap_ref[BD : 2 * BD, :]
    place_wait(waits, recv_ref, newc_ref, sems)


def hidden_kernel(own_ref, r1, r2, r3, w0, w1, w2, w3, out_ref):
    depth = w0.shape[0] - 16
    odd = lax.rem(lax.axis_index("dp"), 2) == 1
    near, far = r1[...].astype(F32), r2[...].astype(F32)
    rows = jnp.concatenate(
        [
            own_ref[...].astype(F32),
            jnp.where(odd, near, far),
            r3[...].astype(F32),
            jnp.where(odd, far, near),
        ],
        axis=0,
    )
    narrow = rows.astype(BF16)
    parts = [
        jnp.dot(narrow, w[0:depth, :], preferred_element_type=F32) for w in (w0, w1, w2, w3)
    ]
    squares = jnp.sum(rows * rows, axis=1, keepdims=True)
    parts.append(jnp.broadcast_to(squares, (rows.shape[0], HD)))
    for k in range(out_ref.shape[0]):
        for i, part in enumerate(parts):
            out_ref[k, :, i * HD : (i + 1) * HD] = part.astype(out_ref.dtype)


def score_kernel(hid_ref, w0, w1, w2, w3, wait_ref, gate_ref, out_ref, gated_ref):
    depth = w0.shape[0] - 16
    total = hid_ref[0].astype(F32)
    for k in range(1, hid_ref.shape[0]):
        total = total + hid_ref[k].astype(F32)
    factor = lax.rsqrt(total[:, 4 * HD : 4 * HD + 1] / D_GEN + 1e-05)
    sums = jnp.zeros((total.shape[0], 1), F32)
    for i, w in enumerate((w0, w1, w2, w3)):
        head = w[depth : depth + 16, :].astype(F32)[0:1, :]
        v = total[:, i * HD : (i + 1) * HD] * factor
        sums = sums + jnp.sum(v / (1.0 + jnp.exp(-v)) * head, axis=1, keepdims=True)
    wide = jnp.broadcast_to(sums, (total.shape[0], HD))
    pairs = out_ref.shape[0] // 2
    mine = lax.rem(lax.axis_index("dp") // 2, pairs)
    for q in range(pairs):
        target = lax.rem(mine + q, pairs)
        for half in range(2):
            out_ref[2 * target + half] = wide[q * BD : (q + 1) * BD]


def final_kernel(meta_ref, part_ref, hop_ref, out_ref, scr):
    total, other = part_ref[0], hop_ref[0]
    for k in range(1, part_ref.shape[0]):
        total = total + part_ref[k]
        other = other + hop_ref[k]
    odd = lax.rem(lax.axis_index("tensor"), 2) == 1
    scr[...] = jnp.where(odd, other, total)
    for s in range(BD):
        rank = meta_ref[BD + s : BD + s + 1, :][0, 0]
        value = scr[pl.ds(jnp.maximum(rank, 0), 1), :][0, 0]
        out_ref[s] = jnp.where(rank >= 0, value, 0.0)


def call(kernel, outs, ins, out_specs, scratch=(), aliases=None, cost=None, limit=60):
    return functools.partial(
        pl.pallas_call,
        kernel,
        out_shape=outs,
        in_specs=[spec(s) for s in ins],
        out_specs=[spec(s) for s in out_specs],
        scratch_shapes=list(scratch),
        input_output_aliases=aliases or {},
        compiler_params=pltpu.CompilerParams(vmem_limit_bytes=limit * 1024 * 1024),
        cost_estimate=pl.CostEstimate(flops=cost or 1000000, bytes_accessed=cost or 1000000, transcendentals=0),
    )()


def shape(dims, dtype):
    return jax.ShapeDtypeStruct(dims, dtype)


def swap(array):
    return lax.ppermute(array, "dp", [(i, i ^ 1) for i in range(lax.axis_size("dp"))])


def swap_half(array, parity):
    nd, nt = lax.axis_size("dp"), lax.axis_size("tensor")
    pairs = [(d * nt + t, (d ^ 1) * nt + t) for d in range(nd) for t in range(parity, nt, 2)]
    return lax.ppermute(array, ("dp", "tensor"), pairs)


def place(first, parity, meta, recv, newc):
    return call(
        functools.partial(place_kernel, first, parity),
        [shape(newc.shape, BF16)],
        [VM, VM, HB],
        [HB],
        [pltpu.SemaphoreType.DMA((BD,))],
        aliases={2: 0},
        limit=16,
    )(meta, recv, newc)[0]


def away(array, nz, k):
    nd = lax.axis_size("dp")
    pairs = []
    for d in range(nd):
        z = d % nz
        pairs.append((d, d - z + (z - k if z % 2 == 0 else z + k) % nz))
    return lax.ppermute(array, "dp", pairs)


def score_groups(nx, nz, nt):
    def index(x, z, t):
        return (x * nz + z) * nt + t

    groups = [[index(x, z, t) for z in range(nz)] for x in range(nx) for t in range(0, nt, 2)]
    across = 2 * nz // nt
    for z in range(nz):
        for x in range(0, nx, across):
            groups.append([index(x + i, z, t) for i in range(across) for t in range(1, nt, 2)])
    return groups


EARLY = 2


def per_device(nx, nz, cache_kv, lengths, step_kv, queries, parents, finished, reward_in, reward_head):
    ndp = nx * nz
    nt = lax.axis_size("tensor")
    cache = cache_kv.reshape(BD, 2, CACHE, HD)
    kv = step_kv.reshape(2, BD, 2, HD)
    depth = reward_in.shape[0]
    part_a = shape((EARLY, 2, CACHE, HD), BF16)
    part_b = shape((MOST - EARLY, 2, CACHE, HD), BF16)
    whole = shape((MOST, 2, CACHE, HD), BF16)
    msg, wext = call(
        message_kernel,
        [shape((BD, 16, HD), BF16), shape((depth + 16, HD), BF16)],
        [SM, VM, VM, HB, VM],
        [VM, VM],
        [pltpu.SemaphoreType.DMA],
        limit=60,
        cost=100000,
    )(finished, queries, kv, reward_in, reward_head.reshape(1, HD))
    recv_msg = swap(msg)
    (oa,) = call(
        pack_kernel,
        [part_a],
        [SM, HB, pl.ANY],
        [VM],
        [pltpu.SemaphoreType.DMA((EARLY,))],
        limit=59,
        cost=20000000,
    )(parents, cache, msg)
    (oa,) = call(
        gate_kernel, [part_a], [pl.ANY, pl.ANY], [pl.ANY], aliases={0: 0}, limit=16, cost=1000
    )(oa, recv_msg)
    recv_oa = swap_half(oa, 1)
    others = [
        lax.ppermute(wext, "dp", [(i, (i + nz * k) % ndp) for i in range(ndp)]) for k in range(1, nx)
    ]
    first_out, own_out, to_swap, rows, meta, to_even, to_odd, newc = call(
        attend_kernel,
        [
            shape((BD, GH * HD), BF16),
            shape((BD, GH * HD), BF16),
            shape((2 * BD, GH * HD), BF16),
            shape((BD, GH * HD), BF16),
            shape((2 * BD, HD), jnp.int32),
            whole,
            part_b,
            shape((BD, 2, CACHE, HD), BF16),
        ],
        [SM, SM, SM, HB, VM, VM, VM],
        [VM] * 7 + [HB],
        [
            VM((BD, 2, CACHE, HD), BF16),
            VM((ALL, HD), F32),
            VM((BD, 2 * GH, HD), BF16),
            VM((ROWS, HD), F32),
            VM((ROWS, HD), F32),
            VM((ALL, HD), jnp.int32),
            VM((OWN, HD), F32),
            VM((ALL, HD), F32),
            VM((2 * BD, GH * HD), F32),
            VM((BD, GH * HD), F32),
            VM((BD, GH * HD), F32),
            pltpu.SemaphoreType.DMA((BD,)),
            pltpu.SemaphoreType.DMA((BD,)),
            pltpu.SemaphoreType.DMA((MOST,)),
        ],
        cost=20000000,
        limit=32,
    )(parents, lengths, finished, cache, queries, kv, recv_msg)
    second_out, rows, to_even, newc = call(
        functools.partial(join_kernel, 1),
        [shape(own_out.shape, BF16), shape(rows.shape, BF16), whole, shape(newc.shape, BF16)],
        [VM] * 5 + [pl.ANY, HB, pl.ANY, pl.ANY, pl.ANY],
        [VM, VM, pl.ANY, HB],
        [pltpu.SemaphoreType.DMA((BD,))],
        aliases={5: 2, 6: 3},
        limit=16,
    )(own_out, rows, swap(to_swap), meta, recv_oa, to_even, newc, *others)
    recv_even = swap_half(to_even, 0)
    (partial,) = call(
        hidden_kernel, [shape((nt, nz // 2 * BD, 5 * HD), BF16)], [VM] * 8, [VM], limit=16
    )(rows, *[away(rows, nz, k) for k in (1, 2, 3)], wext, *others)
    partials = lax.all_to_all(partial, "tensor", 0, 0, tiled=True)
    sums, to_odd = call(
        score_kernel,
        [shape((nz, BD, HD), F32), part_b],
        [VM] * 5 + [pl.ANY, pl.ANY],
        [VM, pl.ANY],
        aliases={6: 1},
        limit=16,
    )(partials, wext, *others, recv_even, to_odd)
    recv_odd = swap_half(to_odd, 1)
    sums = lax.all_to_all(sums, ("dp", "tensor"), 0, 0, axis_index_groups=score_groups(nx, nz, nt), tiled=True)
    hop = lax.ppermute(sums, "tensor", [(t, t + 1) for t in range(0, nt, 2)])
    (scores,) = call(
        final_kernel, [shape((BD,), F32)], [VM, VM, VM], [SM], [VM((BD, HD), F32)], limit=16
    )(meta, sums, hop)
    newc = place(0, 0, meta, recv_even, newc)
    newc = place(EARLY, 1, meta, recv_odd, newc)
    return (first_out, second_out, scores, newc.reshape(cache_kv.shape))


def solution(mesh):
    ndp = mesh.shape["dp"]
    nx = 4
    return jax.shard_map(
        functools.partial(per_device, nx, ndp // nx),
        mesh=mesh,
        in_specs=(
            P("dp", None, None, "tensor", None),
            P(),
            P(None, "dp", None, "tensor", None),
            P(None, "dp", "tensor", None),
            P(),
            P("dp"),
            P("tensor", "dp"),
            P("dp"),
        ),
        out_specs=(
            P("dp", "tensor"),
            P("dp", "tensor"),
            P("dp"),
            P("dp", None, None, "tensor", None),
        ),
        check_vma=False,
    )
```

```python
import functools
import math

import jax
import jax.numpy as jnp
from jax import lax
from jax.experimental import pallas as pl
from jax.experimental.pallas import tpu as pltpu
from jax.sharding import PartitionSpec as P

D_GEN = 8192
MOST = 4
BD = 8
CACHE = 1024
HD = 128
GH = 8
F32 = jnp.float32
BF16 = jnp.bfloat16
VM = pltpu.VMEM
SM = pltpu.SMEM
HB = pltpu.HBM


def spec(space):
    return pl.BlockSpec(memory_space=space)


def needed(par_ref, slots_at, half):
    flags = []
    for b in range(BD):
        want = half * BD + b
        hit = par_ref[slots_at] == want
        for j in range(1, BD):
            hit = hit | (par_ref[slots_at + j] == want)
        flags.append(hit)
    return flags


def ranked(flags):
    ranks = []
    rank = jnp.int32(0)
    for flag in flags:
        ranks.append(rank)
        rank = rank + flag.astype(jnp.int32)
    return ranks, rank


def message_kernel(fin_ref, q_ref, kv_ref, msg_ref):
    for s in range(BD):
        step = kv_ref[1, s].astype(F32)
        flag = jnp.full((1, HD), fin_ref[s], jnp.int32).astype(F32)
        msg_ref[s] = jnp.concatenate(
            [q_ref[1, s].astype(F32), step, flag, jnp.zeros((5, HD), F32)], axis=0
        ).astype(BF16)


def pack_kernel(par_ref, cache_ref, w_ref, head_ref, after_ref, a_ref, wext_ref, sems, wsem):
    me = lax.axis_index("dp")
    half = lax.rem(me, 2)
    start = (me - half) * BD + (1 - half) * BD
    flags = needed(par_ref, start, half)
    ranks, total = ranked(flags)
    early = a_ref.shape[0]
    for b in range(BD):
        for r in range(min(b + 1, early)):

            @pl.when(flags[b] & (ranks[b] == r))
            def _():
                pltpu.make_async_copy(cache_ref.at[b], a_ref.at[r], sems.at[r]).start()

    rows = w_ref.shape[0]
    wcopy = pltpu.make_async_copy(w_ref, wext_ref.at[pl.ds(0, rows)], wsem)
    wcopy.start()
    wext_ref[pl.ds(rows, 16), :] = jnp.broadcast_to(head_ref[...].astype(F32), (16, HD)).astype(BF16)
    wcopy.wait()
    for r in range(early):

        @pl.when(r < total)
        def _():
            pltpu.make_async_copy(cache_ref.at[0], a_ref.at[r], sems.at[r]).wait()


OWN = BD * GH
ALL = OWN + MOST * GH
ROWS = ALL + 2 * GH


def attend_kernel(
    par_ref, len_ref, fin_ref, cache_ref, q_ref, kv_ref, msg_ref,
    first_ref, own_ref, swap_ref, rows_ref, meta_ref, pick_ref, late_ref, newc_ref,
    q2s, q1s, e1s, v1s, pcol, fscr, acc, rscr, crow, outsem, sendsem,
):
    me = lax.axis_index("dp")
    half = lax.rem(me, 2)
    pair = (me - half) * BD
    mine = pair + half * BD
    theirs = pair + (1 - half) * BD
    scaling = math.log2(math.e) / math.sqrt(HD)
    wanted = needed(par_ref, theirs, half)
    send_ranks, send_total = ranked(wanted)
    skip = MOST - late_ref.shape[0]
    for b in range(BD):
        for r in range(skip, min(b + 1, MOST)):

            @pl.when(wanted[b] & (send_ranks[b] == r))
            def _():
                pltpu.make_async_copy(cache_ref.at[b], late_ref.at[r - skip], sendsem.at[r]).start()

    own_local = []
    for s in range(BD):
        local = par_ref[mine + s] - half * BD
        here = (local >= 0) & (local < BD)
        own_local.append(jnp.where(here, local, -1))

        @pl.when(here)
        def _():
            pltpu.make_async_copy(
                cache_ref.at[jnp.clip(local, 0, BD - 1)], newc_ref.at[s], outsem.at[s]
            ).start()

    slots = [jnp.int32(0)] * MOST
    locals_ = [jnp.int32(-1)] * MOST
    count = jnp.int32(0)
    for s in range(BD):
        local = par_ref[theirs + s] - half * BD
        here = (local >= 0) & (local < BD)
        for j in range(min(s + 1, MOST)):
            take = here & (count == j)
            slots[j] = jnp.where(take, s, slots[j])
            locals_[j] = jnp.where(take, local, locals_[j])
        count = count + here.astype(jnp.int32)
    q1s[...] = jnp.zeros_like(q1s)
    for b in range(BD):
        q1s[b, 0:GH, :] = q_ref[0, b]
    e1s[pl.ds(ALL, 2 * GH), :] = jnp.full((2 * GH, HD), -1e30, F32)
    v1s[pl.ds(ALL, 2 * GH), :] = jnp.zeros((2 * GH, HD), F32)
    for s in range(BD + MOST):
        rows = pl.ds(s * GH, GH)
        if s < BD:
            q = q_ref[1, s].astype(F32)
            step = kv_ref[1, s].astype(F32)
            parent = own_local[s]
        else:
            block = msg_ref[slots[s - BD]].astype(F32)
            q = block[0:GH]
            step = block[GH : GH + 2]
            parent = locals_[s - BD]
        pcol[rows, :] = jnp.full((GH, HD), parent, jnp.int32)
        q2s[rows, :] = q
        e1s[rows, :] = jnp.broadcast_to(
            jnp.sum(q * step[0:1], axis=1, keepdims=True) * scaling, (GH, HD)
        )
        v1s[rows, :] = jnp.broadcast_to(step[1:2], (GH, HD))
    q2 = q2s[...].astype(BF16)
    acc[...] = jnp.zeros_like(acc)
    places = lax.broadcasted_iota(jnp.int32, (1, CACHE), 1)
    for b in range(BD):
        bias = jnp.where(places < len_ref[mine + b], 0.0, -1e30)
        q = jnp.concatenate([q2, q1s[b]], axis=0)
        logits = lax.dot_general(
            q, cache_ref[b, 0], (((1,), (1,)), ((), ())), preferred_element_type=F32
        ) * scaling + bias
        step = kv_ref[0, b].astype(F32)
        e0 = jnp.sum(q.astype(F32) * step[0:1], axis=1, keepdims=True) * scaling
        e1 = e1s[:, 0:1]
        peak = jnp.maximum(jnp.maximum(jnp.max(logits, axis=1, keepdims=True), e0), e1)
        p = jnp.exp2(logits - peak)
        p0 = jnp.exp2(e0 - peak)
        p1 = jnp.exp2(e1 - peak)
        inv = 1.0 / (jnp.sum(p, axis=1, keepdims=True) + p0 + p1)
        mixed = jnp.dot((p * inv).astype(BF16), cache_ref[b, 1], preferred_element_type=F32)
        mixed = mixed + (p0 * inv).astype(BF16).astype(F32) * step[1:2]
        mixed = mixed + (p1 * inv).astype(BF16).astype(F32) * v1s[...]
        fscr[b * GH : (b + 1) * GH, :] = mixed[ALL : ALL + GH]
        acc[...] = jnp.where(pcol[...] == b, mixed[:ALL], acc[...])
    rscr[...] = jnp.zeros_like(rscr)
    at = pl.multiple_of(half * BD, BD)
    their = pl.multiple_of((1 - half) * BD, BD)
    for h in range(GH):
        lanes = slice(h * HD, (h + 1) * HD)
        first_ref[:, lanes] = fscr[pl.ds(h, BD, stride=GH), :].astype(BF16)
        rscr[pl.ds(at, BD), lanes] = acc[pl.ds(h, BD, stride=GH), :].astype(BF16).astype(F32)
        crow[0:MOST, lanes] = acc[pl.ds(OWN + h, MOST, stride=GH), :].astype(BF16).astype(F32)
    for j in range(MOST):

        @pl.when(j < count)
        def _():
            rscr[pl.ds(their + slots[j], 1), :] = crow[j : j + 1, :]

    lane = lax.broadcasted_iota(jnp.int32, (BD, HD), 1)
    flags = jnp.zeros((BD, HD), F32)
    for s in range(BD):
        theirs_flag = msg_ref[s].astype(F32)[GH + 2 : GH + 3, :]
        flags = jnp.where(lane == their + s, theirs_flag, flags)
        flags = jnp.where(lane == at + s, fin_ref[s].astype(F32), flags)
    before = flags
    for k in range(4):
        moved = pltpu.roll(before, 1 << k, 1)
        before = before + jnp.where(lane >= 1 << k, moved, 0.0)
    rank = lax.broadcasted_iota(jnp.int32, (BD, HD), 0).astype(F32)
    pick = jnp.where((flags > 0.5) & (before - 1.0 == rank), 1.0, 0.0)
    packed = jnp.dot(
        pick[:, 0 : 2 * BD].astype(BF16), rscr[...].astype(BF16), preferred_element_type=F32
    )
    pick_ref[...] = pltpu.roll(pick, jnp.where(half == 1, HD - BD, 0), 1)
    own_ref[...] = rscr[pl.ds(at, BD), :].astype(BF16)
    rows_ref[...] = packed.astype(BF16)
    swap_ref[...] = jnp.concatenate([rscr[pl.ds(their, BD), :], packed], axis=0).astype(BF16)
    ranks, _ = ranked(needed(par_ref, mine, 1 - half))
    for s in range(BD):
        local = par_ref[mine + s] - (1 - half) * BD
        slot = jnp.int32(-1)
        for b in range(BD):
            slot = jnp.where(local == b, ranks[b], slot)
        meta_ref[s : s + 1, :] = jnp.full((1, HD), slot, jnp.int32)
    for r in range(skip, MOST):

        @pl.when(r < send_total)
        def _():
            pltpu.make_async_copy(cache_ref.at[0], late_ref.at[0], sendsem.at[r]).wait()

    for s in range(BD):

        @pl.when(own_local[s] >= 0)
        def _():
            pltpu.make_async_copy(cache_ref.at[0], newc_ref.at[s], outsem.at[s]).wait()


def place_start(first, meta_ref, recv_ref, newc_ref, sems):
    crossing = []
    count = recv_ref.shape[0]
    for s in range(BD):
        slot = meta_ref[s : s + 1, :][0, 0] - first
        cross = (slot >= 0) & (slot < count)
        slot = jnp.clip(slot, 0, count - 1)
        crossing.append(cross)

        @pl.when(cross)
        def _():
            pltpu.make_async_copy(recv_ref.at[slot], newc_ref.at[s], sems.at[s]).start()

    return crossing


def place_wait(crossing, recv_ref, newc_ref, sems):
    for s in range(BD):

        @pl.when(crossing[s])
        def _():
            pltpu.make_async_copy(recv_ref.at[0], newc_ref.at[s], sems.at[s]).wait()


def place_kernel(first, meta_ref, recv_ref, *refs):
    newc_ref, sems = refs[-2:]
    waits = place_start(first, meta_ref, recv_ref, newc_ref, sems)
    place_wait(waits, recv_ref, newc_ref, sems)


def gate_kernel(*refs):
    del refs


def join_kernel(own_ref, rows_ref, swap_ref, meta_ref, recv_ref, *refs):
    second_ref, full_ref, _, newc_ref, sems = refs[-5:]
    waits = place_start(0, meta_ref, recv_ref, newc_ref, sems)
    second_ref[...] = own_ref[...] + swap_ref[0:BD, :]
    full_ref[...] = rows_ref[...] + swap_ref[BD : 2 * BD, :]
    place_wait(waits, recv_ref, newc_ref, sems)


def hidden_kernel(own_ref, r1, r2, r3, w0, w1, w2, w3, out_ref):
    depth = w0.shape[0] - 16
    odd = lax.rem(lax.axis_index("dp"), 2) == 1
    near, far = r1[...].astype(F32), r2[...].astype(F32)
    rows = jnp.concatenate(
        [
            own_ref[...].astype(F32),
            jnp.where(odd, near, far),
            r3[...].astype(F32),
            jnp.where(odd, far, near),
        ],
        axis=0,
    )
    narrow = rows.astype(BF16)
    parts = [
        jnp.dot(narrow, w[0:depth, :], preferred_element_type=F32) for w in (w0, w1, w2, w3)
    ]
    squares = jnp.sum(rows * rows, axis=1, keepdims=True)
    parts.append(jnp.broadcast_to(squares, (rows.shape[0], HD)))
    for k in range(out_ref.shape[0]):
        for i, part in enumerate(parts):
            out_ref[k, :, i * HD : (i + 1) * HD] = part.astype(out_ref.dtype)


def score_kernel(hid_ref, w0, w1, w2, w3, out_ref):
    depth = w0.shape[0] - 16
    total = hid_ref[0].astype(F32)
    for k in range(1, hid_ref.shape[0]):
        total = total + hid_ref[k].astype(F32)
    factor = lax.rsqrt(total[:, 4 * HD : 4 * HD + 1] / D_GEN + 1e-05)
    sums = jnp.zeros((total.shape[0], 1), F32)
    for i, w in enumerate((w0, w1, w2, w3)):
        head = w[depth : depth + 16, :].astype(F32)[0:1, :]
        v = total[:, i * HD : (i + 1) * HD] * factor
        sums = sums + jnp.sum(v / (1.0 + jnp.exp(-v)) * head, axis=1, keepdims=True)
    wide = jnp.broadcast_to(sums, (total.shape[0], HD))
    pairs = out_ref.shape[0]
    mine = lax.rem(lax.axis_index("dp") // 2, pairs)
    for q in range(pairs):
        out_ref[lax.rem(mine + q, pairs)] = wide[q * BD : (q + 1) * BD]


def add_kernel(a_ref, b_ref, out_ref):
    out_ref[...] = a_ref[...] + b_ref[...]


def final_kernel(pick_ref, a_ref, b_ref, out_ref):
    pair = lax.rem(lax.axis_index("dp") // 2, a_ref.shape[0])
    total = a_ref[pair] + b_ref[pair]
    sums = jnp.sum(pick_ref[...] * total, axis=0, keepdims=True)
    for s in range(BD):
        out_ref[s] = sums[0, s]


def call(kernel, outs, ins, out_specs, scratch=(), aliases=None, cost=None, limit=60):
    return functools.partial(
        pl.pallas_call,
        kernel,
        out_shape=outs,
        in_specs=[spec(s) for s in ins],
        out_specs=[spec(s) for s in out_specs],
        scratch_shapes=list(scratch),
        input_output_aliases=aliases or {},
        compiler_params=pltpu.CompilerParams(vmem_limit_bytes=limit * 1024 * 1024),
        cost_estimate=pl.CostEstimate(flops=cost or 1000000, bytes_accessed=cost or 1000000, transcendentals=0),
    )()


def shape(dims, dtype):
    return jax.ShapeDtypeStruct(dims, dtype)


def swap(array):
    return lax.ppermute(array, "dp", [(i, i ^ 1) for i in range(lax.axis_size("dp"))])


def place(first, meta, recv, newc):
    return call(
        functools.partial(place_kernel, first),
        [shape(newc.shape, BF16)],
        [VM, VM, HB],
        [HB],
        [pltpu.SemaphoreType.DMA((BD,))],
        aliases={2: 0},
        limit=16,
    )(meta, recv, newc)[0]


def away(array, nz, k):
    nd = lax.axis_size("dp")
    pairs = []
    for d in range(nd):
        z = d % nz
        pairs.append((d, d - z + (z - k if z % 2 == 0 else z + k) % nz))
    return lax.ppermute(array, "dp", pairs)


EARLY = 1


def per_device(nx, nz, cache_kv, lengths, step_kv, queries, parents, finished, reward_in, reward_head):
    ndp = nx * nz
    nt = lax.axis_size("tensor")
    cache = cache_kv.reshape(BD, 2, CACHE, HD)
    kv = step_kv.reshape(2, BD, 2, HD)
    depth = reward_in.shape[0]
    part_a = shape((EARLY, 2, CACHE, HD), BF16)
    part_b = shape((MOST - EARLY, 2, CACHE, HD), BF16)
    (msg,) = call(
        message_kernel, [shape((BD, 16, HD), BF16)], [SM, VM, VM], [VM], limit=60, cost=100000
    )(finished, queries, kv)
    recv_msg = swap(msg)
    early, wext = call(
        pack_kernel,
        [part_a, shape((depth + 16, HD), BF16)],
        [SM, HB, HB, VM, pl.ANY],
        [VM, VM],
        [pltpu.SemaphoreType.DMA((EARLY,)), pltpu.SemaphoreType.DMA],
        limit=58,
        cost=20000000,
    )(parents, cache, reward_in, reward_head.reshape(1, HD), msg)
    (early,) = call(
        gate_kernel, [part_a], [pl.ANY, pl.ANY], [pl.ANY], aliases={0: 0}, limit=16, cost=1000
    )(early, recv_msg)
    recv_early = swap(early)
    others = [
        lax.ppermute(wext, "dp", [(i, (i + nz * k) % ndp) for i in range(ndp)]) for k in range(1, nx)
    ]
    first_out, own_out, to_swap, rows, meta, pick, late, newc = call(
        attend_kernel,
        [
            shape((BD, GH * HD), BF16),
            shape((BD, GH * HD), BF16),
            shape((2 * BD, GH * HD), BF16),
            shape((BD, GH * HD), BF16),
            shape((BD, HD), jnp.int32),
            shape((BD, HD), F32),
            part_b,
            shape((BD, 2, CACHE, HD), BF16),
        ],
        [SM, SM, SM, VM, VM, VM, VM],
        [VM] * 7 + [HB],
        [
            VM((ALL, HD), F32),
            VM((BD, 2 * GH, HD), BF16),
            VM((ROWS, HD), F32),
            VM((ROWS, HD), F32),
            VM((ALL, HD), jnp.int32),
            VM((OWN, HD), F32),
            VM((ALL, HD), F32),
            VM((2 * BD, GH * HD), F32),
            VM((BD, GH * HD), F32),
            pltpu.SemaphoreType.DMA((BD,)),
            pltpu.SemaphoreType.DMA((MOST,)),
        ],
        cost=20000000,
        limit=32,
    )(parents, lengths, finished, cache, queries, kv, recv_msg)
    second_out, rows, late, newc = call(
        join_kernel,
        [shape(own_out.shape, BF16), shape(rows.shape, BF16), part_b, shape(newc.shape, BF16)],
        [VM] * 5 + [pl.ANY, HB, pl.ANY, pl.ANY, pl.ANY],
        [VM, VM, pl.ANY, HB],
        [pltpu.SemaphoreType.DMA((BD,))],
        aliases={5: 2, 6: 3},
        limit=16,
    )(own_out, rows, swap(to_swap), meta, recv_early, late, newc, *others)
    recv_late = swap(late)
    (partial,) = call(
        hidden_kernel, [shape((nt, nz // 2 * BD, 5 * HD), BF16)], [VM] * 8, [VM], limit=16
    )(rows, *[away(rows, nz, k) for k in (1, 2, 3)], wext, *others)
    partials = lax.all_to_all(partial, "tensor", 0, 0, tiled=True)
    (sums,) = call(
        score_kernel, [shape((nz // 2, BD, HD), F32)], [VM] * 5, [VM], limit=16
    )(partials, wext, *others)
    for k in (1, 2):
        (sums,) = call(add_kernel, [shape(sums.shape, F32)], [VM, VM], [VM], limit=16)(
            sums, away(sums, nz, k)
        )
    (scores,) = call(
        final_kernel, [shape((BD,), F32)], [VM, VM, VM], [SM], limit=16
    )(pick, sums, away(sums, nz, 3))
    newc = place(EARLY, meta, recv_late, newc)
    return (first_out, second_out, scores, newc.reshape(cache_kv.shape))


def solution(mesh):
    ndp = mesh.shape["dp"]
    nx = 4
    return jax.shard_map(
        functools.partial(per_device, nx, ndp // nx),
        mesh=mesh,
        in_specs=(
            P("dp", None, None, "tensor", None),
            P(),
            P(None, "dp", None, "tensor", None),
            P(None, "dp", "tensor", None),
            P(),
            P("dp"),
            P("tensor", "dp"),
            P("dp"),
        ),
        out_specs=(
            P("dp", "tensor"),
            P("dp", "tensor"),
            P("dp"),
            P("dp", None, None, "tensor", None),
        ),
        check_vma=False,
    )
```

```python
import functools
import math

import jax
import jax.numpy as jnp
from jax import lax
from jax.experimental import pallas as pl
from jax.experimental.pallas import tpu as pltpu
from jax.sharding import PartitionSpec as P

D_GEN = 8192
MOST = 4
BD = 8
CACHE = 1024
HD = 128
GH = 8
F32 = jnp.float32
BF16 = jnp.bfloat16
VM = pltpu.VMEM
SM = pltpu.SMEM
HB = pltpu.HBM


def spec(space):
    return pl.BlockSpec(memory_space=space)


def locals_of(par_ref, slots_at, half):
    found = []
    for j in range(BD):
        local = par_ref[slots_at + j] - half * BD
        found.append(jnp.where((local >= 0) & (local < BD), local, -1))
    return found


def needed(found):
    mask = jnp.int32(0)
    for local in found:
        mask = mask | jnp.where(local >= 0, jnp.int32(1) << jnp.maximum(local, 0), 0)
    ranks, beams = [], [jnp.int32(0)] * MOST
    total = jnp.int32(0)
    for b in range(BD):
        bit = (mask >> b) & 1
        ranks.append(total)
        for r in range(min(b + 1, MOST)):
            beams[r] = jnp.where((bit == 1) & (total == r), b, beams[r])
        total = total + bit
    return ranks, beams, total


def message_kernel(fin_ref, q_ref, kv_ref, msg_ref):
    for s in range(BD):
        step = kv_ref[1, s].astype(F32)
        flag = jnp.full((1, HD), fin_ref[s], jnp.int32).astype(F32)
        msg_ref[s] = jnp.concatenate(
            [q_ref[1, s].astype(F32), step, flag, jnp.zeros((5, HD), F32)], axis=0
        ).astype(BF16)


def pack_kernel(par_ref, cache_ref, w_ref, head_ref, after_ref, a_ref, wext_ref, sems, wsem):
    me = lax.axis_index("dp")
    half = lax.rem(me, 2)
    start = (me - half) * BD + (1 - half) * BD
    _, beams, total = needed(locals_of(par_ref, start, half))
    early = a_ref.shape[0]
    for u in range(early):

        @pl.when(u // 2 < total)
        def _():
            pltpu.make_async_copy(cache_ref.at[beams[u // 2], u % 2], a_ref.at[u], sems.at[u]).start()

    rows = w_ref.shape[0]
    wcopy = pltpu.make_async_copy(w_ref, wext_ref.at[pl.ds(0, rows)], wsem)
    wcopy.start()
    wext_ref[pl.ds(rows, 16), :] = jnp.broadcast_to(head_ref[...].astype(F32), (16, HD)).astype(BF16)
    wcopy.wait()
    for u in range(early):

        @pl.when(u // 2 < total)
        def _():
            pltpu.make_async_copy(cache_ref.at[0, 0], a_ref.at[u], sems.at[u]).wait()


OWN = BD * GH
ALL = OWN + MOST * GH
ROWS = ALL + 2 * GH


def attend_kernel(
    par_ref, len_ref, fin_ref, cache_ref, q_ref, kv_ref, msg_ref,
    first_ref, own_ref, swap_ref, rows_ref, meta_ref, pick_ref, late_ref, newc_ref,
    q2s, q1s, e1s, v1s, pcol, fscr, acc, rscr, crow, outsem, sendsem,
):
    me = lax.axis_index("dp")
    half = lax.rem(me, 2)
    pair = (me - half) * BD
    mine = pair + half * BD
    theirs = pair + (1 - half) * BD
    scaling = math.log2(math.e) / math.sqrt(HD)
    their_local = locals_of(par_ref, theirs, half)
    _, beams, send_total = needed(their_local)
    skip = 2 * MOST - late_ref.shape[0]
    for u in range(skip, 2 * MOST):

        @pl.when(u // 2 < send_total)
        def _():
            pltpu.make_async_copy(
                cache_ref.at[beams[u // 2], u % 2], late_ref.at[u - skip], sendsem.at[u]
            ).start()

    own_local = locals_of(par_ref, mine, half)
    for s in range(BD):

        @pl.when(own_local[s] >= 0)
        def _():
            pltpu.make_async_copy(
                cache_ref.at[jnp.maximum(own_local[s], 0)], newc_ref.at[s], outsem.at[s]
            ).start()

    slots = [jnp.int32(0)] * MOST
    locals_ = [jnp.int32(-1)] * MOST
    count = jnp.int32(0)
    for s in range(BD):
        here = their_local[s] >= 0
        for j in range(min(s + 1, MOST)):
            take = here & (count == j)
            slots[j] = jnp.where(take, s, slots[j])
            locals_[j] = jnp.where(take, their_local[s], locals_[j])
        count = count + here.astype(jnp.int32)
    q1s[...] = jnp.zeros_like(q1s)
    for b in range(BD):
        q1s[b, 0:GH, :] = q_ref[0, b]
    e1s[pl.ds(ALL, 2 * GH), :] = jnp.full((2 * GH, HD), -1e30, F32)
    v1s[pl.ds(ALL, 2 * GH), :] = jnp.zeros((2 * GH, HD), F32)
    for s in range(BD + MOST):
        rows = pl.ds(s * GH, GH)
        if s < BD:
            q = q_ref[1, s].astype(F32)
            step = kv_ref[1, s].astype(F32)
            parent = own_local[s]
        else:
            block = msg_ref[slots[s - BD]].astype(F32)
            q = block[0:GH]
            step = block[GH : GH + 2]
            parent = locals_[s - BD]
        pcol[rows, :] = jnp.full((GH, HD), parent, jnp.int32)
        q2s[rows, :] = q
        e1s[rows, :] = jnp.broadcast_to(
            jnp.sum(q * step[0:1], axis=1, keepdims=True) * scaling, (GH, HD)
        )
        v1s[rows, :] = jnp.broadcast_to(step[1:2], (GH, HD))
    q2 = q2s[...].astype(BF16)
    acc[...] = jnp.zeros_like(acc)
    places = lax.broadcasted_iota(jnp.int32, (1, CACHE), 1)
    for b in range(BD):
        bias = jnp.where(places < len_ref[mine + b], 0.0, -1e30)
        q = jnp.concatenate([q2, q1s[b]], axis=0)
        logits = lax.dot_general(
            q, cache_ref[b, 0], (((1,), (1,)), ((), ())), preferred_element_type=F32
        ) * scaling + bias
        step = kv_ref[0, b].astype(F32)
        e0 = jnp.sum(q.astype(F32) * step[0:1], axis=1, keepdims=True) * scaling
        e1 = e1s[:, 0:1]
        peak = jnp.maximum(jnp.maximum(jnp.max(logits, axis=1, keepdims=True), e0), e1)
        p = jnp.exp2(logits - peak)
        p0 = jnp.exp2(e0 - peak)
        p1 = jnp.exp2(e1 - peak)
        inv = 1.0 / (jnp.sum(p, axis=1, keepdims=True) + p0 + p1)
        mixed = jnp.dot(p.astype(BF16), cache_ref[b, 1], preferred_element_type=F32)
        mixed = (mixed + p0 * step[1:2] + p1 * v1s[...]) * inv
        fscr[b * GH : (b + 1) * GH, :] = mixed[ALL : ALL + GH]
        acc[...] = jnp.where(pcol[...] == b, mixed[:ALL], acc[...])
    rscr[...] = jnp.zeros_like(rscr)
    at = pl.multiple_of(half * BD, BD)
    their = pl.multiple_of((1 - half) * BD, BD)
    for h in range(GH):
        lanes = slice(h * HD, (h + 1) * HD)
        first_ref[:, lanes] = fscr[pl.ds(h, BD, stride=GH), :].astype(BF16)
        rscr[pl.ds(at, BD), lanes] = acc[pl.ds(h, BD, stride=GH), :].astype(BF16).astype(F32)
        crow[0:MOST, lanes] = acc[pl.ds(OWN + h, MOST, stride=GH), :].astype(BF16).astype(F32)
    for j in range(MOST):

        @pl.when(j < count)
        def _():
            rscr[pl.ds(their + slots[j], 1), :] = crow[j : j + 1, :]

    lane = lax.broadcasted_iota(jnp.int32, (BD, HD), 1)
    flags = jnp.zeros((BD, HD), F32)
    for s in range(BD):
        theirs_flag = msg_ref[s].astype(F32)[GH + 2 : GH + 3, :]
        flags = jnp.where(lane == their + s, theirs_flag, flags)
        flags = jnp.where(lane == at + s, fin_ref[s].astype(F32), flags)
    before = flags
    for k in range(4):
        moved = pltpu.roll(before, 1 << k, 1)
        before = before + jnp.where(lane >= 1 << k, moved, 0.0)
    rank = lax.broadcasted_iota(jnp.int32, (BD, HD), 0).astype(F32)
    pick = jnp.where((flags > 0.5) & (before - 1.0 == rank), 1.0, 0.0)
    packed = jnp.dot(
        pick[:, 0 : 2 * BD].astype(BF16), rscr[...].astype(BF16), preferred_element_type=F32
    )
    pick_ref[...] = pltpu.roll(pick, jnp.where(half == 1, HD - BD, 0), 1)
    own_ref[...] = rscr[pl.ds(at, BD), :].astype(BF16)
    rows_ref[...] = packed.astype(BF16)
    swap_ref[...] = jnp.concatenate([rscr[pl.ds(their, BD), :], packed], axis=0).astype(BF16)
    cross_local = locals_of(par_ref, mine, 1 - half)
    ranks, _, _ = needed(cross_local)
    for s in range(BD):
        slot = jnp.int32(-1)
        for b in range(BD):
            slot = jnp.where(cross_local[s] == b, ranks[b], slot)
        meta_ref[s : s + 1, :] = jnp.full((1, HD), slot, jnp.int32)
    for u in range(skip, 2 * MOST):

        @pl.when(u // 2 < send_total)
        def _():
            pltpu.make_async_copy(cache_ref.at[0, 0], late_ref.at[0], sendsem.at[u]).wait()

    for s in range(BD):

        @pl.when(own_local[s] >= 0)
        def _():
            pltpu.make_async_copy(cache_ref.at[0], newc_ref.at[s], outsem.at[s]).wait()


def place_kernel(first, meta_ref, recv_ref, pick_ref, *refs):
    token_ref, newc_ref, sems = refs[-3:]
    token_ref[...] = pick_ref[...]
    count = recv_ref.shape[0]
    waits = []
    for s in range(BD):
        slot = meta_ref[s : s + 1, :][0, 0]
        for half in range(2):
            unit = 2 * slot + half - first
            fits = (slot >= 0) & (unit >= 0) & (unit < count)
            waits.append(fits)

            @pl.when(fits)
            def _():
                pltpu.make_async_copy(
                    recv_ref.at[jnp.clip(unit, 0, count - 1)], newc_ref.at[s, half], sems.at[s, half]
                ).start()

    for s in range(BD):
        for half in range(2):

            @pl.when(waits[2 * s + half])
            def _():
                pltpu.make_async_copy(recv_ref.at[0], newc_ref.at[s, half], sems.at[s, half]).wait()


def gate_kernel(*refs):
    del refs


def join_kernel(own_ref, rows_ref, swap_ref, *refs):
    second_ref, full_ref = refs[-3:-1]
    second_ref[...] = own_ref[...] + swap_ref[0:BD, :]
    full_ref[...] = rows_ref[...] + swap_ref[BD : 2 * BD, :]


def hidden_kernel(own_ref, r1, r2, r3, w0, w1, w2, w3, out_ref):
    depth = w0.shape[0] - 16
    odd = lax.rem(lax.axis_index("dp"), 2) == 1
    near, far = r1[...].astype(F32), r2[...].astype(F32)
    rows = jnp.concatenate(
        [
            own_ref[...].astype(F32),
            jnp.where(odd, near, far),
            r3[...].astype(F32),
            jnp.where(odd, far, near),
        ],
        axis=0,
    )
    narrow = rows.astype(BF16)
    parts = [
        jnp.dot(narrow, w[0:depth, :], preferred_element_type=F32) for w in (w0, w1, w2, w3)
    ]
    squares = jnp.sum(rows * rows, axis=1, keepdims=True)
    parts.append(jnp.broadcast_to(squares, (rows.shape[0], HD)))
    for k in range(out_ref.shape[0]):
        for i, part in enumerate(parts):
            out_ref[k, :, i * HD : (i + 1) * HD] = part.astype(out_ref.dtype)


def score_kernel(hid_ref, w0, w1, w2, w3, out_ref):
    depth = w0.shape[0] - 16
    total = hid_ref[0].astype(F32)
    for k in range(1, hid_ref.shape[0]):
        total = total + hid_ref[k].astype(F32)
    factor = lax.rsqrt(total[:, 4 * HD : 4 * HD + 1] / D_GEN + 1e-05)
    sums = jnp.zeros((total.shape[0], 1), F32)
    for i, w in enumerate((w0, w1, w2, w3)):
        head = w[depth : depth + 16, :].astype(F32)[0:1, :]
        v = total[:, i * HD : (i + 1) * HD] * factor
        sums = sums + jnp.sum(v / (1.0 + jnp.exp(-v)) * head, axis=1, keepdims=True)
    wide = jnp.broadcast_to(sums, (total.shape[0], HD))
    pairs = out_ref.shape[0]
    mine = lax.rem(lax.axis_index("dp") // 2, pairs)
    for q in range(pairs):
        out_ref[lax.rem(mine + q, pairs)] = wide[q * BD : (q + 1) * BD]


def spread_kernel(own_ref, near_ref, far_ref, two_ref, three_ref):
    two_ref[...] = near_ref[...] + far_ref[...]
    three_ref[...] = own_ref[...] + two_ref[...]


def final_kernel(pick_ref, own_ref, two_ref, three_ref, out_ref):
    pair = lax.rem(lax.axis_index("dp") // 2, own_ref.shape[0])
    total = own_ref[pair] + two_ref[pair] + three_ref[pair]
    sums = jnp.sum(pick_ref[...] * total, axis=0, keepdims=True)
    for s in range(BD):
        out_ref[s] = sums[0, s]


def call(kernel, outs, ins, out_specs, scratch=(), aliases=None, cost=None, limit=60):
    return functools.partial(
        pl.pallas_call,
        kernel,
        out_shape=outs,
        in_specs=[spec(s) for s in ins],
        out_specs=[spec(s) for s in out_specs],
        scratch_shapes=list(scratch),
        input_output_aliases=aliases or {},
        compiler_params=pltpu.CompilerParams(vmem_limit_bytes=limit * 1024 * 1024),
        cost_estimate=pl.CostEstimate(flops=cost or 1000000, bytes_accessed=cost or 1000000, transcendentals=0),
    )()


def shape(dims, dtype):
    return jax.ShapeDtypeStruct(dims, dtype)


def swap(array):
    return lax.ppermute(array, "dp", [(i, i ^ 1) for i in range(lax.axis_size("dp"))])


def place(first, meta, recv, pick, newc):
    return call(
        functools.partial(place_kernel, first),
        [shape(pick.shape, F32), shape(newc.shape, BF16)],
        [VM, VM, VM, HB],
        [VM, HB],
        [pltpu.SemaphoreType.DMA((BD, 2))],
        aliases={3: 1},
        limit=16,
    )(meta, recv, pick, newc)


def away(array, nz, k):
    nd = lax.axis_size("dp")
    pairs = []
    for d in range(nd):
        z = d % nz
        pairs.append((d, d - z + (z - k if z % 2 == 0 else z + k) % nz))
    return lax.ppermute(array, "dp", pairs)


EARLY = 1


def per_device(nx, nz, cache_kv, lengths, step_kv, queries, parents, finished, reward_in, reward_head):
    ndp = nx * nz
    nt = lax.axis_size("tensor")
    cache = cache_kv.reshape(BD, 2, CACHE, HD)
    kv = step_kv.reshape(2, BD, 2, HD)
    depth = reward_in.shape[0]
    part_a = shape((EARLY, CACHE, HD), BF16)
    part_b = shape((2 * MOST - EARLY, CACHE, HD), BF16)
    (msg,) = call(
        message_kernel, [shape((BD, 16, HD), BF16)], [SM, VM, VM], [VM], limit=57, cost=100000
    )(finished, queries, kv)
    recv_msg = swap(msg)
    early, wext = call(
        pack_kernel,
        [part_a, shape((depth + 16, HD), BF16)],
        [SM, HB, HB, VM, pl.ANY],
        [VM, VM],
        [pltpu.SemaphoreType.DMA((EARLY,)), pltpu.SemaphoreType.DMA],
        limit=57,
        cost=20000000,
    )(parents, cache, reward_in, reward_head.reshape(1, HD), msg)
    (early,) = call(
        gate_kernel, [part_a], [pl.ANY, pl.ANY], [pl.ANY], aliases={0: 0}, limit=16, cost=1000
    )(early, recv_msg)
    recv_early = swap(early)
    others = [
        lax.ppermute(wext, "dp", [(i, (i + nz * k) % ndp) for i in range(ndp)]) for k in range(1, nx)
    ]
    first_out, own_out, to_swap, rows, meta, pick, late, newc = call(
        attend_kernel,
        [
            shape((BD, GH * HD), BF16),
            shape((BD, GH * HD), BF16),
            shape((2 * BD, GH * HD), BF16),
            shape((BD, GH * HD), BF16),
            shape((BD, HD), jnp.int32),
            shape((BD, HD), F32),
            part_b,
            shape((BD, 2, CACHE, HD), BF16),
        ],
        [SM, SM, SM, VM, VM, VM, VM],
        [VM] * 7 + [HB],
        [
            VM((ALL, HD), F32),
            VM((BD, 2 * GH, HD), BF16),
            VM((ROWS, HD), F32),
            VM((ROWS, HD), F32),
            VM((ALL, HD), jnp.int32),
            VM((OWN, HD), F32),
            VM((ALL, HD), F32),
            VM((2 * BD, GH * HD), F32),
            VM((BD, GH * HD), F32),
            pltpu.SemaphoreType.DMA((BD,)),
            pltpu.SemaphoreType.DMA((2 * MOST,)),
        ],
        cost=20000000,
        limit=32,
    )(parents, lengths, finished, cache, queries, kv, recv_msg)
    second_out, rows, late = call(
        join_kernel,
        [shape(own_out.shape, BF16), shape(rows.shape, BF16), part_b],
        [VM] * 3 + [pl.ANY] * 4,
        [VM, VM, pl.ANY],
        aliases={3: 2},
        limit=16,
    )(own_out, rows, swap(to_swap), late, recv_early, others[0], others[2])
    recv_late = swap(late)
    (partial,) = call(
        hidden_kernel, [shape((nt, nz // 2 * BD, 5 * HD), BF16)], [VM] * 8, [VM], limit=16
    )(rows, *[away(rows, nz, k) for k in (1, 2, 3)], wext, *others)
    partials = lax.all_to_all(partial, "tensor", 0, 0, tiled=True)
    (sums,) = call(
        score_kernel, [shape((nz // 2, BD, HD), F32)], [VM] * 5, [VM], limit=16
    )(partials, wext, *others)
    two, three = call(
        spread_kernel, [shape(sums.shape, F32)] * 2, [VM] * 3, [VM] * 2, limit=16
    )(sums, away(sums, nz, 1), away(sums, nz, 2))
    pick, newc = place(0, meta, recv_early, pick, newc)
    pick, newc = place(EARLY, meta, recv_late, pick, newc)
    (scores,) = call(
        final_kernel, [shape((BD,), F32)], [VM] * 4, [SM], limit=16
    )(pick, three, away(two, nz, 2), away(three, nz, 3))
    return (first_out, second_out, scores, newc.reshape(cache_kv.shape))


def solution(mesh):
    ndp = mesh.shape["dp"]
    nx = 4
    return jax.shard_map(
        functools.partial(per_device, nx, ndp // nx),
        mesh=mesh,
        in_specs=(
            P("dp", None, None, "tensor", None),
            P(),
            P(None, "dp", None, "tensor", None),
            P(None, "dp", "tensor", None),
            P(),
            P("dp"),
            P("tensor", "dp"),
            P("dp"),
        ),
        out_specs=(
            P("dp", "tensor"),
            P("dp", "tensor"),
            P("dp"),
            P("dp", None, None, "tensor", None),
        ),
        check_vma=False,
    )
```

```python
import functools
import math

import jax
import jax.numpy as jnp
from jax import lax
from jax.experimental import pallas as pl
from jax.experimental.pallas import tpu as pltpu
from jax.sharding import PartitionSpec as P

D_GEN = 8192
MOST = 4
BD = 8
CACHE = 1024
HD = 128
GH = 8
F32 = jnp.float32
BF16 = jnp.bfloat16
VM = pltpu.VMEM
SM = pltpu.SMEM
HB = pltpu.HBM


def spec(space):
    return pl.BlockSpec(memory_space=space)


def locals_of(par_ref, slots_at, half):
    found = []
    for j in range(BD):
        local = par_ref[slots_at + j] - half * BD
        found.append(jnp.where((local >= 0) & (local < BD), local, -1))
    return found


def needed(found):
    mask = jnp.int32(0)
    for local in found:
        mask = mask | jnp.where(local >= 0, jnp.int32(1) << jnp.maximum(local, 0), 0)
    ranks, beams = [], [jnp.int32(0)] * MOST
    total = jnp.int32(0)
    for b in range(BD):
        bit = (mask >> b) & 1
        ranks.append(total)
        for r in range(min(b + 1, MOST)):
            beams[r] = jnp.where((bit == 1) & (total == r), b, beams[r])
        total = total + bit
    return ranks, beams, total


def message_kernel(fin_ref, q_ref, kv_ref, msg_ref):
    for s in range(BD):
        step = kv_ref[1, s].astype(F32)
        flag = jnp.full((1, HD), fin_ref[s], jnp.int32).astype(F32)
        msg_ref[s] = jnp.concatenate(
            [q_ref[1, s].astype(F32), step, flag, jnp.zeros((5, HD), F32)], axis=0
        ).astype(BF16)


def pack_kernel(par_ref, cache_ref, w_ref, head_ref, after_ref, a_ref, wext_ref, sems, wsem):
    me = lax.axis_index("dp")
    half = lax.rem(me, 2)
    start = (me - half) * BD + (1 - half) * BD
    _, beams, total = needed(locals_of(par_ref, start, half))
    early = a_ref.shape[0]
    for u in range(early):

        @pl.when(u // 2 < total)
        def _():
            pltpu.make_async_copy(cache_ref.at[beams[u // 2], u % 2], a_ref.at[u], sems.at[u]).start()

    rows = w_ref.shape[0]
    wcopy = pltpu.make_async_copy(w_ref, wext_ref.at[pl.ds(0, rows)], wsem)
    wcopy.start()
    wext_ref[pl.ds(rows, 16), :] = jnp.broadcast_to(head_ref[...].astype(F32), (16, HD)).astype(BF16)
    wcopy.wait()
    for u in range(early):

        @pl.when(u // 2 < total)
        def _():
            pltpu.make_async_copy(cache_ref.at[0, 0], a_ref.at[u], sems.at[u]).wait()


OWN = BD * GH
ALL = OWN + MOST * GH
ROWS = ALL + 2 * GH


def attend_kernel(
    par_ref, len_ref, fin_ref, cache_ref, q_ref, kv_ref, msg_ref,
    first_ref, own_ref, swap_ref, rows_ref, meta_ref, pick_ref, late_ref, newc_ref,
    q2s, q1s, e1s, v1s, pcol, fscr, acc, rscr, crow, outsem, sendsem,
):
    me = lax.axis_index("dp")
    half = lax.rem(me, 2)
    pair = (me - half) * BD
    mine = pair + half * BD
    theirs = pair + (1 - half) * BD
    scaling = math.log2(math.e) / math.sqrt(HD)
    their_local = locals_of(par_ref, theirs, half)
    _, beams, send_total = needed(their_local)
    skip = 2 * MOST - late_ref.shape[0]
    for u in range(skip, 2 * MOST):

        @pl.when(u // 2 < send_total)
        def _():
            pltpu.make_async_copy(
                cache_ref.at[beams[u // 2], u % 2], late_ref.at[u - skip], sendsem.at[u]
            ).start()

    own_local = locals_of(par_ref, mine, half)
    for s in range(BD):

        @pl.when(own_local[s] >= 0)
        def _():
            pltpu.make_async_copy(
                cache_ref.at[jnp.maximum(own_local[s], 0)], newc_ref.at[s], outsem.at[s]
            ).start()

    slots = [jnp.int32(0)] * MOST
    locals_ = [jnp.int32(-1)] * MOST
    count = jnp.int32(0)
    for s in range(BD):
        here = their_local[s] >= 0
        for j in range(min(s + 1, MOST)):
            take = here & (count == j)
            slots[j] = jnp.where(take, s, slots[j])
            locals_[j] = jnp.where(take, their_local[s], locals_[j])
        count = count + here.astype(jnp.int32)
    q1s[...] = jnp.zeros_like(q1s)
    for b in range(BD):
        q1s[b, 0:GH, :] = q_ref[0, b]
    e1s[pl.ds(ALL, 2 * GH), :] = jnp.full((2 * GH, HD), -1e30, F32)
    v1s[pl.ds(ALL, 2 * GH), :] = jnp.zeros((2 * GH, HD), F32)
    for s in range(BD + MOST):
        rows = pl.ds(s * GH, GH)
        if s < BD:
            q = q_ref[1, s].astype(F32)
            step = kv_ref[1, s].astype(F32)
            parent = own_local[s]
        else:
            block = msg_ref[slots[s - BD]].astype(F32)
            q = block[0:GH]
            step = block[GH : GH + 2]
            parent = locals_[s - BD]
        pcol[rows, :] = jnp.full((GH, HD), parent, jnp.int32)
        q2s[rows, :] = q
        e1s[rows, :] = jnp.broadcast_to(
            jnp.sum(q * step[0:1], axis=1, keepdims=True) * scaling, (GH, HD)
        )
        v1s[rows, :] = jnp.broadcast_to(step[1:2], (GH, HD))
    q2 = q2s[...].astype(BF16)
    acc[...] = jnp.zeros_like(acc)
    places = lax.broadcasted_iota(jnp.int32, (1, CACHE), 1)
    def match(b):
        q = jnp.concatenate([q2, q1s[b]], axis=0)
        return q, lax.dot_general(
            q, cache_ref[b, 0], (((1,), (1,)), ((), ())), preferred_element_type=F32
        )

    def weigh(b, q, logits):
        bias = jnp.where(places < len_ref[mine + b], 0.0, -1e30)
        logits = logits * scaling + bias
        step = kv_ref[0, b].astype(F32)
        e0 = jnp.sum(q.astype(F32) * step[0:1], axis=1, keepdims=True) * scaling
        e1 = e1s[:, 0:1]
        peak = jnp.maximum(jnp.maximum(jnp.max(logits, axis=1, keepdims=True), e0), e1)
        p = jnp.exp2(logits - peak)
        p0 = jnp.exp2(e0 - peak)
        p1 = jnp.exp2(e1 - peak)
        inv = 1.0 / (jnp.sum(p, axis=1, keepdims=True) + p0 + p1)
        return p, p0, p1, inv, step

    def mix(b, p, p0, p1, inv, step):
        mixed = jnp.dot((p * inv).astype(BF16), cache_ref[b, 1], preferred_element_type=F32)
        mixed = mixed + (p0 * inv).astype(BF16).astype(F32) * step[1:2]
        mixed = mixed + (p1 * inv).astype(BF16).astype(F32) * v1s[...]
        fscr[b * GH : (b + 1) * GH, :] = mixed[ALL : ALL + GH]
        acc[...] = jnp.where(pcol[...] == b, mixed[:ALL], acc[...])

    first = match(0)
    second = match(1)
    held = weigh(0, *first)
    for b in range(BD):
        third = match(b + 2) if b + 2 < BD else None
        ahead = weigh(b + 1, *second) if b + 1 < BD else None
        mix(b, *held)
        held, second = ahead, third
    rscr[...] = jnp.zeros_like(rscr)
    at = pl.multiple_of(half * BD, BD)
    their = pl.multiple_of((1 - half) * BD, BD)
    for h in range(GH):
        lanes = slice(h * HD, (h + 1) * HD)
        first_ref[:, lanes] = fscr[pl.ds(h, BD, stride=GH), :].astype(BF16)
        rscr[pl.ds(at, BD), lanes] = acc[pl.ds(h, BD, stride=GH), :].astype(BF16).astype(F32)
        crow[0:MOST, lanes] = acc[pl.ds(OWN + h, MOST, stride=GH), :].astype(BF16).astype(F32)
    for j in range(MOST):

        @pl.when(j < count)
        def _():
            rscr[pl.ds(their + slots[j], 1), :] = crow[j : j + 1, :]

    lane = lax.broadcasted_iota(jnp.int32, (BD, HD), 1)
    flags = jnp.zeros((BD, HD), F32)
    for s in range(BD):
        theirs_flag = msg_ref[s].astype(F32)[GH + 2 : GH + 3, :]
        flags = jnp.where(lane == their + s, theirs_flag, flags)
        flags = jnp.where(lane == at + s, fin_ref[s].astype(F32), flags)
    before = flags
    for k in range(4):
        moved = pltpu.roll(before, 1 << k, 1)
        before = before + jnp.where(lane >= 1 << k, moved, 0.0)
    rank = lax.broadcasted_iota(jnp.int32, (BD, HD), 0).astype(F32)
    pick = jnp.where((flags > 0.5) & (before - 1.0 == rank), 1.0, 0.0)
    packed = jnp.dot(
        pick[:, 0 : 2 * BD].astype(BF16), rscr[...].astype(BF16), preferred_element_type=F32
    )
    pick_ref[...] = pltpu.roll(pick, jnp.where(half == 1, HD - BD, 0), 1)
    own_ref[...] = rscr[pl.ds(at, BD), :].astype(BF16)
    rows_ref[...] = packed.astype(BF16)
    swap_ref[...] = jnp.concatenate([rscr[pl.ds(their, BD), :], packed], axis=0).astype(BF16)
    cross_local = locals_of(par_ref, mine, 1 - half)
    ranks, _, _ = needed(cross_local)
    for s in range(BD):
        slot = jnp.int32(-1)
        for b in range(BD):
            slot = jnp.where(cross_local[s] == b, ranks[b], slot)
        meta_ref[s : s + 1, :] = jnp.full((1, HD), slot, jnp.int32)
    for u in range(skip, 2 * MOST):

        @pl.when(u // 2 < send_total)
        def _():
            pltpu.make_async_copy(cache_ref.at[0, 0], late_ref.at[0], sendsem.at[u]).wait()

    for s in range(BD):

        @pl.when(own_local[s] >= 0)
        def _():
            pltpu.make_async_copy(cache_ref.at[0], newc_ref.at[s], outsem.at[s]).wait()


def place_kernel(first, meta_ref, recv_ref, pick_ref, *refs):
    token_ref, newc_ref, sems = refs[-3:]
    token_ref[...] = pick_ref[...]
    count = recv_ref.shape[0]
    waits = []
    for s in range(BD):
        slot = meta_ref[s : s + 1, :][0, 0]
        for half in range(2):
            unit = 2 * slot + half - first
            fits = (slot >= 0) & (unit >= 0) & (unit < count)
            waits.append(fits)

            @pl.when(fits)
            def _():
                pltpu.make_async_copy(
                    recv_ref.at[jnp.clip(unit, 0, count - 1)], newc_ref.at[s, half], sems.at[s, half]
                ).start()

    for s in range(BD):
        for half in range(2):

            @pl.when(waits[2 * s + half])
            def _():
                pltpu.make_async_copy(recv_ref.at[0], newc_ref.at[s, half], sems.at[s, half]).wait()


def gate_kernel(*refs):
    del refs


def join_kernel(own_ref, rows_ref, swap_ref, *refs):
    second_ref, full_ref = refs[-3:-1]
    second_ref[...] = own_ref[...] + swap_ref[0:BD, :]
    full_ref[...] = rows_ref[...] + swap_ref[BD : 2 * BD, :]


def hidden_kernel(own_ref, r1, r2, r3, w0, w1, w2, w3, out_ref):
    depth = w0.shape[0] - 16
    odd = lax.rem(lax.axis_index("dp"), 2) == 1
    near, far = r1[...].astype(F32), r2[...].astype(F32)
    rows = jnp.concatenate(
        [
            own_ref[...].astype(F32),
            jnp.where(odd, near, far),
            r3[...].astype(F32),
            jnp.where(odd, far, near),
        ],
        axis=0,
    )
    narrow = rows.astype(BF16)
    parts = [
        jnp.dot(narrow, w[0:depth, :], preferred_element_type=F32) for w in (w0, w1, w2, w3)
    ]
    squares = jnp.sum(rows * rows, axis=1, keepdims=True)
    parts.append(jnp.broadcast_to(squares, (rows.shape[0], HD)))
    for k in range(out_ref.shape[0]):
        for i, part in enumerate(parts):
            out_ref[k, :, i * HD : (i + 1) * HD] = part.astype(out_ref.dtype)


def score_kernel(hid_ref, w0, w1, w2, w3, out_ref):
    depth = w0.shape[0] - 16
    total = hid_ref[0].astype(F32)
    for k in range(1, hid_ref.shape[0]):
        total = total + hid_ref[k].astype(F32)
    factor = lax.rsqrt(total[:, 4 * HD : 4 * HD + 1] / D_GEN + 1e-05)
    sums = jnp.zeros((total.shape[0], 1), F32)
    for i, w in enumerate((w0, w1, w2, w3)):
        head = w[depth : depth + 16, :].astype(F32)[0:1, :]
        v = total[:, i * HD : (i + 1) * HD] * factor
        sums = sums + jnp.sum(v / (1.0 + jnp.exp(-v)) * head, axis=1, keepdims=True)
    wide = jnp.broadcast_to(sums, (total.shape[0], HD))
    pairs = out_ref.shape[0]
    mine = lax.rem(lax.axis_index("dp") // 2, pairs)
    for q in range(pairs):
        out_ref[lax.rem(mine + q, pairs)] = wide[q * BD : (q + 1) * BD]


def spread_kernel(own_ref, near_ref, far_ref, two_ref, three_ref):
    two_ref[...] = near_ref[...] + far_ref[...]
    three_ref[...] = own_ref[...] + two_ref[...]


def final_kernel(pick_ref, own_ref, two_ref, three_ref, out_ref):
    pair = lax.rem(lax.axis_index("dp") // 2, own_ref.shape[0])
    total = own_ref[pair] + two_ref[pair] + three_ref[pair]
    sums = jnp.sum(pick_ref[...] * total, axis=0, keepdims=True)
    for s in range(BD):
        out_ref[s] = sums[0, s]


def call(kernel, outs, ins, out_specs, scratch=(), aliases=None, cost=None, limit=60):
    return functools.partial(
        pl.pallas_call,
        kernel,
        out_shape=outs,
        in_specs=[spec(s) for s in ins],
        out_specs=[spec(s) for s in out_specs],
        scratch_shapes=list(scratch),
        input_output_aliases=aliases or {},
        compiler_params=pltpu.CompilerParams(vmem_limit_bytes=limit * 1024 * 1024),
        cost_estimate=pl.CostEstimate(flops=cost or 1000000, bytes_accessed=cost or 1000000, transcendentals=0),
    )()


def shape(dims, dtype):
    return jax.ShapeDtypeStruct(dims, dtype)


def swap(array):
    return lax.ppermute(array, "dp", [(i, i ^ 1) for i in range(lax.axis_size("dp"))])


def place(first, meta, recv, pick, newc):
    return call(
        functools.partial(place_kernel, first),
        [shape(pick.shape, F32), shape(newc.shape, BF16)],
        [VM, VM, VM, HB],
        [VM, HB],
        [pltpu.SemaphoreType.DMA((BD, 2))],
        aliases={3: 1},
        limit=16,
    )(meta, recv, pick, newc)


def away(array, nz, k):
    nd = lax.axis_size("dp")
    pairs = []
    for d in range(nd):
        z = d % nz
        pairs.append((d, d - z + (z - k if z % 2 == 0 else z + k) % nz))
    return lax.ppermute(array, "dp", pairs)


EARLY = 1


def per_device(nx, nz, cache_kv, lengths, step_kv, queries, parents, finished, reward_in, reward_head):
    ndp = nx * nz
    nt = lax.axis_size("tensor")
    cache = cache_kv.reshape(BD, 2, CACHE, HD)
    kv = step_kv.reshape(2, BD, 2, HD)
    depth = reward_in.shape[0]
    part_a = shape((EARLY, CACHE, HD), BF16)
    part_b = shape((2 * MOST - EARLY, CACHE, HD), BF16)
    (msg,) = call(
        message_kernel, [shape((BD, 16, HD), BF16)], [SM, VM, VM], [VM], limit=57, cost=100000
    )(finished, queries, kv)
    recv_msg = swap(msg)
    early, wext = call(
        pack_kernel,
        [part_a, shape((depth + 16, HD), BF16)],
        [SM, HB, HB, VM, pl.ANY],
        [VM, VM],
        [pltpu.SemaphoreType.DMA((EARLY,)), pltpu.SemaphoreType.DMA],
        limit=57,
        cost=20000000,
    )(parents, cache, reward_in, reward_head.reshape(1, HD), msg)
    (early,) = call(
        gate_kernel, [part_a], [pl.ANY, pl.ANY], [pl.ANY], aliases={0: 0}, limit=16, cost=1000
    )(early, recv_msg)
    recv_early = swap(early)
    others = [
        lax.ppermute(wext, "dp", [(i, (i + nz * k) % ndp) for i in range(ndp)]) for k in range(1, nx)
    ]
    first_out, own_out, to_swap, rows, meta, pick, late, newc = call(
        attend_kernel,
        [
            shape((BD, GH * HD), BF16),
            shape((BD, GH * HD), BF16),
            shape((2 * BD, GH * HD), BF16),
            shape((BD, GH * HD), BF16),
            shape((BD, HD), jnp.int32),
            shape((BD, HD), F32),
            part_b,
            shape((BD, 2, CACHE, HD), BF16),
        ],
        [SM, SM, SM, VM, VM, VM, VM],
        [VM] * 7 + [HB],
        [
            VM((ALL, HD), F32),
            VM((BD, 2 * GH, HD), BF16),
            VM((ROWS, HD), F32),
            VM((ROWS, HD), F32),
            VM((ALL, HD), jnp.int32),
            VM((OWN, HD), F32),
            VM((ALL, HD), F32),
            VM((2 * BD, GH * HD), F32),
            VM((BD, GH * HD), F32),
            pltpu.SemaphoreType.DMA((BD,)),
            pltpu.SemaphoreType.DMA((2 * MOST,)),
        ],
        cost=20000000,
        limit=32,
    )(parents, lengths, finished, cache, queries, kv, recv_msg)
    second_out, rows, late = call(
        join_kernel,
        [shape(own_out.shape, BF16), shape(rows.shape, BF16), part_b],
        [VM] * 3 + [pl.ANY] * 4,
        [VM, VM, pl.ANY],
        aliases={3: 2},
        limit=16,
    )(own_out, rows, swap(to_swap), late, recv_early, others[0], others[2])
    recv_late = swap(late)
    (partial,) = call(
        hidden_kernel, [shape((nt, nz // 2 * BD, 5 * HD), BF16)], [VM] * 8, [VM], limit=16
    )(rows, *[away(rows, nz, k) for k in (1, 2, 3)], wext, *others)
    partials = lax.all_to_all(partial, "tensor", 0, 0, tiled=True)
    (sums,) = call(
        score_kernel, [shape((nz // 2, BD, HD), F32)], [VM] * 5, [VM], limit=16
    )(partials, wext, *others)
    two, three = call(
        spread_kernel, [shape(sums.shape, F32)] * 2, [VM] * 3, [VM] * 2, limit=16
    )(sums, away(sums, nz, 1), away(sums, nz, 2))
    pick, newc = place(0, meta, recv_early, pick, newc)
    pick, newc = place(EARLY, meta, recv_late, pick, newc)
    (scores,) = call(
        final_kernel, [shape((BD,), F32)], [VM] * 4, [SM], limit=16
    )(pick, three, away(two, nz, 2), away(three, nz, 3))
    return (first_out, second_out, scores, newc.reshape(cache_kv.shape))


def solution(mesh):
    ndp = mesh.shape["dp"]
    nx = 4
    return jax.shard_map(
        functools.partial(per_device, nx, ndp // nx),
        mesh=mesh,
        in_specs=(
            P("dp", None, None, "tensor", None),
            P(),
            P(None, "dp", None, "tensor", None),
            P(None, "dp", "tensor", None),
            P(),
            P("dp"),
            P("tensor", "dp"),
            P("dp"),
        ),
        out_specs=(
            P("dp", "tensor"),
            P("dp", "tensor"),
            P("dp"),
            P("dp", None, None, "tensor", None),
        ),
        check_vma=False,
    )
```

```python
import functools
import math

import jax
import jax.numpy as jnp
from jax import lax
from jax.experimental import pallas as pl
from jax.experimental.pallas import tpu as pltpu
from jax.sharding import PartitionSpec as P

D_GEN = 8192
MOST = 4
BD = 8
CACHE = 1024
HD = 128
GH = 8
F32 = jnp.float32
BF16 = jnp.bfloat16
VM = pltpu.VMEM
SM = pltpu.SMEM
HB = pltpu.HBM


def spec(space):
    return pl.BlockSpec(memory_space=space)


def locals_of(par_ref, slots_at, half):
    found = []
    for j in range(BD):
        local = par_ref[slots_at + j] - half * BD
        found.append(jnp.where((local >= 0) & (local < BD), local, -1))
    return found


def needed(found):
    mask = jnp.int32(0)
    for local in found:
        mask = mask | jnp.where(local >= 0, jnp.int32(1) << jnp.maximum(local, 0), 0)
    ranks, beams = [], [jnp.int32(0)] * MOST
    total = jnp.int32(0)
    for b in range(BD):
        bit = (mask >> b) & 1
        ranks.append(total)
        for r in range(min(b + 1, MOST)):
            beams[r] = jnp.where((bit == 1) & (total == r), b, beams[r])
        total = total + bit
    return ranks, beams, total


def pack_kernel(
    par_ref, fin_ref, cache_ref, w_ref, head_ref, q_ref, kv_ref, msg_ref, a_ref, wext_ref, sems, wsem
):
    me = lax.axis_index("dp")
    half = lax.rem(me, 2)
    start = (me - half) * BD + (1 - half) * BD
    rows = w_ref.shape[0]
    wcopy = pltpu.make_async_copy(w_ref, wext_ref.at[pl.ds(0, rows)], wsem)
    wcopy.start()
    _, beams, total = needed(locals_of(par_ref, start, half))
    early = a_ref.shape[0]
    for u in range(early):

        @pl.when(u // 2 < total)
        def _():
            pltpu.make_async_copy(cache_ref.at[beams[u // 2], u % 2], a_ref.at[u], sems.at[u]).start()

    wext_ref[pl.ds(rows, 16), :] = jnp.broadcast_to(head_ref[...].astype(F32), (16, HD)).astype(BF16)
    for s in range(BD):
        step = kv_ref[1, s].astype(F32)
        flag = jnp.full((1, HD), fin_ref[s], jnp.int32).astype(F32)
        msg_ref[s] = jnp.concatenate(
            [q_ref[1, s].astype(F32), step, flag, jnp.zeros((5, HD), F32)], axis=0
        ).astype(BF16)
    wcopy.wait()
    for u in range(early):

        @pl.when(u // 2 < total)
        def _():
            pltpu.make_async_copy(cache_ref.at[0, 0], a_ref.at[u], sems.at[u]).wait()


OWN = BD * GH
ALL = OWN + MOST * GH
ROWS = ALL + 2 * GH


def attend_kernel(
    par_ref, len_ref, fin_ref, cache_ref, q_ref, kv_ref, msg_ref,
    first_ref, own_ref, swap_ref, rows_ref, meta_ref, pick_ref, late_ref, newc_ref,
    q2s, q1s, e1s, v1s, pcol, fscr, acc, rscr, crow, outsem, sendsem,
):
    me = lax.axis_index("dp")
    half = lax.rem(me, 2)
    pair = (me - half) * BD
    mine = pair + half * BD
    theirs = pair + (1 - half) * BD
    scaling = math.log2(math.e) / math.sqrt(HD)
    their_local = locals_of(par_ref, theirs, half)
    _, beams, send_total = needed(their_local)
    skip = 2 * MOST - late_ref.shape[0]
    for u in range(skip, 2 * MOST):

        @pl.when(u // 2 < send_total)
        def _():
            pltpu.make_async_copy(
                cache_ref.at[beams[u // 2], u % 2], late_ref.at[u - skip], sendsem.at[u]
            ).start()

    own_local = locals_of(par_ref, mine, half)
    for s in range(BD):

        @pl.when(own_local[s] >= 0)
        def _():
            pltpu.make_async_copy(
                cache_ref.at[jnp.maximum(own_local[s], 0)], newc_ref.at[s], outsem.at[s]
            ).start()

    slots = [jnp.int32(0)] * MOST
    locals_ = [jnp.int32(-1)] * MOST
    count = jnp.int32(0)
    for s in range(BD):
        here = their_local[s] >= 0
        for j in range(min(s + 1, MOST)):
            take = here & (count == j)
            slots[j] = jnp.where(take, s, slots[j])
            locals_[j] = jnp.where(take, their_local[s], locals_[j])
        count = count + here.astype(jnp.int32)
    q1s[...] = jnp.zeros_like(q1s)
    for b in range(BD):
        q1s[b, 0:GH, :] = q_ref[0, b]
    e1s[pl.ds(ALL, 2 * GH), :] = jnp.full((2 * GH, HD), -1e30, F32)
    v1s[pl.ds(ALL, 2 * GH), :] = jnp.zeros((2 * GH, HD), F32)
    for s in range(BD + MOST):
        rows = pl.ds(s * GH, GH)
        if s < BD:
            q = q_ref[1, s].astype(F32)
            step = kv_ref[1, s].astype(F32)
            parent = own_local[s]
        else:
            block = msg_ref[slots[s - BD]].astype(F32)
            q = block[0:GH]
            step = block[GH : GH + 2]
            parent = locals_[s - BD]
        pcol[rows, :] = jnp.full((GH, HD), parent, jnp.int32)
        q2s[rows, :] = q
        e1s[rows, :] = jnp.broadcast_to(
            jnp.sum(q * step[0:1], axis=1, keepdims=True) * scaling, (GH, HD)
        )
        v1s[rows, :] = jnp.broadcast_to(step[1:2], (GH, HD))
    q2 = q2s[...].astype(BF16)
    acc[...] = jnp.zeros_like(acc)
    places = lax.broadcasted_iota(jnp.int32, (1, CACHE), 1)
    def match(b):
        q = jnp.concatenate([q2, q1s[b]], axis=0)
        return q, lax.dot_general(
            q, cache_ref[b, 0], (((1,), (1,)), ((), ())), preferred_element_type=F32
        )

    def weigh(b, q, logits):
        bias = jnp.where(places < len_ref[mine + b], 0.0, -1e30)
        logits = logits * scaling + bias
        step = kv_ref[0, b].astype(F32)
        e0 = jnp.sum(q.astype(F32) * step[0:1], axis=1, keepdims=True) * scaling
        e1 = e1s[:, 0:1]
        peak = jnp.maximum(jnp.maximum(jnp.max(logits, axis=1, keepdims=True), e0), e1)
        p = jnp.exp2(logits - peak)
        p0 = jnp.exp2(e0 - peak)
        p1 = jnp.exp2(e1 - peak)
        inv = 1.0 / (jnp.sum(p, axis=1, keepdims=True) + p0 + p1)
        return p, p0, p1, inv, step

    def mix(b, p, p0, p1, inv, step):
        mixed = jnp.dot((p * inv).astype(BF16), cache_ref[b, 1], preferred_element_type=F32)
        mixed = mixed + (p0 * inv).astype(BF16).astype(F32) * step[1:2]
        mixed = mixed + (p1 * inv).astype(BF16).astype(F32) * v1s[...]
        fscr[b * GH : (b + 1) * GH, :] = mixed[ALL : ALL + GH]
        acc[...] = jnp.where(pcol[...] == b, mixed[:ALL], acc[...])

    first = match(0)
    second = match(1)
    held = weigh(0, *first)
    for b in range(BD):
        third = match(b + 2) if b + 2 < BD else None
        ahead = weigh(b + 1, *second) if b + 1 < BD else None
        mix(b, *held)
        held, second = ahead, third
    rscr[...] = jnp.zeros_like(rscr)
    at = pl.multiple_of(half * BD, BD)
    their = pl.multiple_of((1 - half) * BD, BD)
    for h in range(GH):
        lanes = slice(h * HD, (h + 1) * HD)
        first_ref[:, lanes] = fscr[pl.ds(h, BD, stride=GH), :].astype(BF16)
        rscr[pl.ds(at, BD), lanes] = acc[pl.ds(h, BD, stride=GH), :].astype(BF16).astype(F32)
        crow[0:MOST, lanes] = acc[pl.ds(OWN + h, MOST, stride=GH), :].astype(BF16).astype(F32)
    for j in range(MOST):

        @pl.when(j < count)
        def _():
            rscr[pl.ds(their + slots[j], 1), :] = crow[j : j + 1, :]

    lane = lax.broadcasted_iota(jnp.int32, (BD, HD), 1)
    flags = jnp.zeros((BD, HD), F32)
    for s in range(BD):
        theirs_flag = msg_ref[s].astype(F32)[GH + 2 : GH + 3, :]
        flags = jnp.where(lane == their + s, theirs_flag, flags)
        flags = jnp.where(lane == at + s, fin_ref[s].astype(F32), flags)
    before = flags
    for k in range(4):
        moved = pltpu.roll(before, 1 << k, 1)
        before = before + jnp.where(lane >= 1 << k, moved, 0.0)
    rank = lax.broadcasted_iota(jnp.int32, (BD, HD), 0).astype(F32)
    pick = jnp.where((flags > 0.5) & (before - 1.0 == rank), 1.0, 0.0)
    packed = jnp.dot(
        pick[:, 0 : 2 * BD].astype(BF16), rscr[...].astype(BF16), preferred_element_type=F32
    )
    pick_ref[...] = pltpu.roll(pick, jnp.where(half == 1, HD - BD, 0), 1)
    own_ref[...] = rscr[pl.ds(at, BD), :].astype(BF16)
    rows_ref[...] = packed.astype(BF16)
    swap_ref[...] = jnp.concatenate([rscr[pl.ds(their, BD), :], packed], axis=0).astype(BF16)
    cross_local = locals_of(par_ref, mine, 1 - half)
    ranks, _, _ = needed(cross_local)
    for s in range(BD):
        slot = jnp.int32(-1)
        for b in range(BD):
            slot = jnp.where(cross_local[s] == b, ranks[b], slot)
        meta_ref[s : s + 1, :] = jnp.full((1, HD), slot, jnp.int32)
    for u in range(skip, 2 * MOST):

        @pl.when(u // 2 < send_total)
        def _():
            pltpu.make_async_copy(cache_ref.at[0, 0], late_ref.at[0], sendsem.at[u]).wait()

    for s in range(BD):

        @pl.when(own_local[s] >= 0)
        def _():
            pltpu.make_async_copy(cache_ref.at[0], newc_ref.at[s], outsem.at[s]).wait()


def place_kernel(first, meta_ref, recv_ref, pick_ref, *refs):
    token_ref, newc_ref, sems = refs[-3:]
    token_ref[...] = pick_ref[...]
    count = recv_ref.shape[0]
    waits = []
    for s in range(BD):
        slot = meta_ref[s : s + 1, :][0, 0]
        for half in range(2):
            unit = 2 * slot + half - first
            fits = (slot >= 0) & (unit >= 0) & (unit < count)
            waits.append(fits)

            @pl.when(fits)
            def _():
                pltpu.make_async_copy(
                    recv_ref.at[jnp.clip(unit, 0, count - 1)], newc_ref.at[s, half], sems.at[s, half]
                ).start()

    for s in range(BD):
        for half in range(2):

            @pl.when(waits[2 * s + half])
            def _():
                pltpu.make_async_copy(recv_ref.at[0], newc_ref.at[s, half], sems.at[s, half]).wait()


def gate_kernel(*refs):
    del refs


def join_kernel(own_ref, rows_ref, swap_ref, *refs):
    second_ref, full_ref = refs[-3:-1]
    second_ref[...] = own_ref[...] + swap_ref[0:BD, :]
    full_ref[...] = rows_ref[...] + swap_ref[BD : 2 * BD, :]


def hidden_kernel(own_ref, r1, r2, r3, w0, w1, w2, w3, out_ref):
    depth = w0.shape[0] - 16
    odd = lax.rem(lax.axis_index("dp"), 2) == 1
    near, far = r1[...].astype(F32), r2[...].astype(F32)
    rows = jnp.concatenate(
        [
            own_ref[...].astype(F32),
            jnp.where(odd, near, far),
            r3[...].astype(F32),
            jnp.where(odd, far, near),
        ],
        axis=0,
    )
    narrow = rows.astype(BF16)
    parts = [
        jnp.dot(narrow, w[0:depth, :], preferred_element_type=F32) for w in (w0, w1, w2, w3)
    ]
    squares = jnp.sum(rows * rows, axis=1, keepdims=True)
    parts.append(jnp.broadcast_to(squares, (rows.shape[0], HD)))
    for k in range(out_ref.shape[0]):
        for i, part in enumerate(parts):
            out_ref[k, :, i * HD : (i + 1) * HD] = part.astype(out_ref.dtype)


def score_kernel(hid_ref, w0, w1, w2, w3, out_ref):
    depth = w0.shape[0] - 16
    total = hid_ref[0].astype(F32)
    for k in range(1, hid_ref.shape[0]):
        total = total + hid_ref[k].astype(F32)
    factor = lax.rsqrt(total[:, 4 * HD : 4 * HD + 1] / D_GEN + 1e-05)
    sums = jnp.zeros((total.shape[0], 1), F32)
    for i, w in enumerate((w0, w1, w2, w3)):
        head = w[depth : depth + 16, :].astype(F32)[0:1, :]
        v = total[:, i * HD : (i + 1) * HD] * factor
        sums = sums + jnp.sum(v / (1.0 + jnp.exp(-v)) * head, axis=1, keepdims=True)
    wide = jnp.broadcast_to(sums, (total.shape[0], HD))
    pairs = out_ref.shape[0]
    mine = lax.rem(lax.axis_index("dp") // 2, pairs)
    for q in range(pairs):
        out_ref[lax.rem(mine + q, pairs)] = wide[q * BD : (q + 1) * BD]


def spread_kernel(own_ref, near_ref, far_ref, two_ref, three_ref):
    two_ref[...] = near_ref[...] + far_ref[...]
    three_ref[...] = own_ref[...] + two_ref[...]


def final_kernel(pick_ref, own_ref, two_ref, three_ref, out_ref):
    pair = lax.rem(lax.axis_index("dp") // 2, own_ref.shape[0])
    total = own_ref[pair] + two_ref[pair] + three_ref[pair]
    sums = jnp.sum(pick_ref[...] * total, axis=0, keepdims=True)
    for s in range(BD):
        out_ref[s] = sums[0, s]


def call(kernel, outs, ins, out_specs, scratch=(), aliases=None, cost=None, limit=60):
    return functools.partial(
        pl.pallas_call,
        kernel,
        out_shape=outs,
        in_specs=[spec(s) for s in ins],
        out_specs=[spec(s) for s in out_specs],
        scratch_shapes=list(scratch),
        input_output_aliases=aliases or {},
        compiler_params=pltpu.CompilerParams(vmem_limit_bytes=limit * 1024 * 1024),
        cost_estimate=pl.CostEstimate(flops=cost or 1000000, bytes_accessed=cost or 1000000, transcendentals=0),
    )()


def shape(dims, dtype):
    return jax.ShapeDtypeStruct(dims, dtype)


def swap(array):
    return lax.ppermute(array, "dp", [(i, i ^ 1) for i in range(lax.axis_size("dp"))])


def place(first, meta, recv, pick, newc):
    return call(
        functools.partial(place_kernel, first),
        [shape(pick.shape, F32), shape(newc.shape, BF16)],
        [VM, VM, VM, HB],
        [VM, HB],
        [pltpu.SemaphoreType.DMA((BD, 2))],
        aliases={3: 1},
        limit=16,
    )(meta, recv, pick, newc)


def away(array, nz, k):
    nd = lax.axis_size("dp")
    pairs = []
    for d in range(nd):
        z = d % nz
        pairs.append((d, d - z + (z - k if z % 2 == 0 else z + k) % nz))
    return lax.ppermute(array, "dp", pairs)


EARLY = 1


def per_device(nx, nz, cache_kv, lengths, step_kv, queries, parents, finished, reward_in, reward_head):
    ndp = nx * nz
    nt = lax.axis_size("tensor")
    cache = cache_kv.reshape(BD, 2, CACHE, HD)
    kv = step_kv.reshape(2, BD, 2, HD)
    depth = reward_in.shape[0]
    part_a = shape((EARLY, CACHE, HD), BF16)
    part_b = shape((2 * MOST - EARLY, CACHE, HD), BF16)
    msg, early, wext = call(
        pack_kernel,
        [shape((BD, 16, HD), BF16), part_a, shape((depth + 16, HD), BF16)],
        [SM, SM, HB, HB, VM, VM, VM],
        [VM, VM, VM],
        [pltpu.SemaphoreType.DMA((EARLY,)), pltpu.SemaphoreType.DMA],
        limit=57,
        cost=1000000,
    )(parents, finished, cache, reward_in, reward_head.reshape(1, HD), queries, kv)
    recv_msg = swap(msg)
    (early,) = call(
        gate_kernel, [part_a], [pl.ANY, pl.ANY], [pl.ANY], aliases={0: 0}, limit=16, cost=1000
    )(early, recv_msg)
    recv_early = swap(early)
    near_w, far_w = (
        lax.ppermute(wext, "dp", [(i, (i + nz * k) % ndp) for i in range(ndp)]) for k in (1, nx - 1)
    )
    others = [near_w, lax.ppermute(near_w, "dp", [(i, (i + nz) % ndp) for i in range(ndp)]), far_w]
    first_out, own_out, to_swap, rows, meta, pick, late, newc = call(
        attend_kernel,
        [
            shape((BD, GH * HD), BF16),
            shape((BD, GH * HD), BF16),
            shape((2 * BD, GH * HD), BF16),
            shape((BD, GH * HD), BF16),
            shape((BD, HD), jnp.int32),
            shape((BD, HD), F32),
            part_b,
            shape((BD, 2, CACHE, HD), BF16),
        ],
        [SM, SM, SM, VM, VM, VM, VM],
        [VM] * 7 + [HB],
        [
            VM((ALL, HD), F32),
            VM((BD, 2 * GH, HD), BF16),
            VM((ROWS, HD), F32),
            VM((ROWS, HD), F32),
            VM((ALL, HD), jnp.int32),
            VM((OWN, HD), F32),
            VM((ALL, HD), F32),
            VM((2 * BD, GH * HD), F32),
            VM((BD, GH * HD), F32),
            pltpu.SemaphoreType.DMA((BD,)),
            pltpu.SemaphoreType.DMA((2 * MOST,)),
        ],
        cost=20000000,
        limit=32,
    )(parents, lengths, finished, cache, queries, kv, recv_msg)
    second_out, rows, late = call(
        join_kernel,
        [shape(own_out.shape, BF16), shape(rows.shape, BF16), part_b],
        [VM] * 3 + [pl.ANY] * 4,
        [VM, VM, pl.ANY],
        aliases={3: 2},
        limit=16,
    )(own_out, rows, swap(to_swap), late, recv_early, others[0], others[2])
    recv_late = swap(late)
    (partial,) = call(
        hidden_kernel, [shape((nt, nz // 2 * BD, 5 * HD), BF16)], [VM] * 8, [VM], limit=16
    )(rows, *[away(rows, nz, k) for k in (1, 2, 3)], wext, *others)
    partials = lax.all_to_all(partial, "tensor", 0, 0, tiled=True)
    (sums,) = call(
        score_kernel, [shape((nz // 2, BD, HD), F32)], [VM] * 5, [VM], limit=16
    )(partials, wext, *others)
    two, three = call(
        spread_kernel, [shape(sums.shape, F32)] * 2, [VM] * 3, [VM] * 2, limit=16
    )(sums, away(sums, nz, 1), away(sums, nz, 2))
    pick, newc = place(0, meta, recv_early, pick, newc)
    pick, newc = place(EARLY, meta, recv_late, pick, newc)
    (scores,) = call(
        final_kernel, [shape((BD,), F32)], [VM] * 4, [SM], limit=16
    )(pick, three, away(two, nz, 2), away(three, nz, 3))
    return (first_out, second_out, scores, newc.reshape(cache_kv.shape))


def solution(mesh):
    ndp = mesh.shape["dp"]
    nx = 4
    return jax.shard_map(
        functools.partial(per_device, nx, ndp // nx),
        mesh=mesh,
        in_specs=(
            P("dp", None, None, "tensor", None),
            P(),
            P(None, "dp", None, "tensor", None),
            P(None, "dp", "tensor", None),
            P(),
            P("dp"),
            P("tensor", "dp"),
            P("dp"),
        ),
        out_specs=(
            P("dp", "tensor"),
            P("dp", "tensor"),
            P("dp"),
            P("dp", None, None, "tensor", None),
        ),
        check_vma=False,
    )
```

```python
import functools
import math

import jax
import jax.numpy as jnp
from jax import lax
from jax.experimental import pallas as pl
from jax.experimental.pallas import tpu as pltpu
from jax.sharding import PartitionSpec as P

D_GEN = 8192
MOST = 4
PARTS = 4
BD = 8
CACHE = 1024
HD = 128
GH = 8
F32 = jnp.float32
BF16 = jnp.bfloat16
VM = pltpu.VMEM
SM = pltpu.SMEM
HB = pltpu.HBM


def spec(space):
    return pl.BlockSpec(memory_space=space)


def locals_of(par_ref, slots_at, half):
    found = []
    for j in range(BD):
        local = par_ref[slots_at + j] - half * BD
        found.append(jnp.where((local >= 0) & (local < BD), local, -1))
    return found


def needed(found):
    mask = jnp.int32(0)
    for local in found:
        mask = mask | jnp.where(local >= 0, jnp.int32(1) << jnp.maximum(local, 0), 0)
    ranks, beams = [], [jnp.int32(0)] * MOST
    total = jnp.int32(0)
    for b in range(BD):
        bit = (mask >> b) & 1
        ranks.append(total)
        for r in range(min(b + 1, MOST)):
            beams[r] = jnp.where((bit == 1) & (total == r), b, beams[r])
        total = total + bit
    return ranks, beams, total


def pack_kernel(
    par_ref, fin_ref, cache_ref, w_ref, head_ref, q_ref, kv_ref, msg_ref, a_ref, wext_ref, sem, wsem
):
    me = lax.axis_index("dp")
    half = lax.rem(me, 2)
    start = (me - half) * BD + (1 - half) * BD
    rows = w_ref.shape[0]
    wcopy = pltpu.make_async_copy(w_ref, wext_ref.at[pl.ds(0, rows)], wsem)
    wcopy.start()
    _, beams, total = needed(locals_of(par_ref, start, half))
    early = a_ref.shape[0]

    @pl.when(total > 0)
    def _():
        pltpu.make_async_copy(cache_ref.at[beams[0], pl.ds(0, early)], a_ref, sem).start()

    wext_ref[pl.ds(rows, 16), :] = jnp.broadcast_to(head_ref[...].astype(F32), (16, HD)).astype(BF16)
    for s in range(BD):
        step = kv_ref[1, s].astype(F32)
        flag = jnp.full((1, HD), fin_ref[s], jnp.int32).astype(F32)
        msg_ref[s] = jnp.concatenate(
            [q_ref[1, s].astype(F32), step, flag, jnp.zeros((5, HD), F32)], axis=0
        ).astype(BF16)
    wcopy.wait()

    @pl.when(total > 0)
    def _():
        pltpu.make_async_copy(cache_ref.at[0, pl.ds(0, early)], a_ref, sem).wait()


OWN = BD * GH
ALL = OWN + MOST * GH
ROWS = ALL + 2 * GH


def attend_kernel(
    par_ref, len_ref, fin_ref, cache_ref, q_ref, kv_ref, msg_ref,
    first_ref, own_ref, swap_ref, rows_ref, meta_ref, pick_ref, late_ref, newc_ref,
    q2s, q1s, e1s, v1s, pcol, fscr, acc, rscr, crow, outsem, sendsem,
):
    me = lax.axis_index("dp")
    half = lax.rem(me, 2)
    pair = (me - half) * BD
    mine = pair + half * BD
    theirs = pair + (1 - half) * BD
    scaling = math.log2(math.e) / math.sqrt(HD)
    their_local = locals_of(par_ref, theirs, half)
    _, beams, send_total = needed(their_local)
    skip = MOST * PARTS - late_ref.shape[0]

    def late_copy(r):
        low = skip if r == 0 else 0
        return pltpu.make_async_copy(
            cache_ref.at[beams[r], pl.ds(low, PARTS - low)],
            late_ref.at[pl.ds(r * PARTS + low - skip, PARTS - low)],
            sendsem.at[r],
        )

    for r in range(MOST):

        @pl.when(r < send_total)
        def _():
            late_copy(r).start()

    own_local = locals_of(par_ref, mine, half)
    for s in range(BD):

        @pl.when(own_local[s] >= 0)
        def _():
            pltpu.make_async_copy(
                cache_ref.at[jnp.maximum(own_local[s], 0)], newc_ref.at[s], outsem.at[s]
            ).start()

    slots = [jnp.int32(0)] * MOST
    locals_ = [jnp.int32(-1)] * MOST
    count = jnp.int32(0)
    for s in range(BD):
        here = their_local[s] >= 0
        for j in range(min(s + 1, MOST)):
            take = here & (count == j)
            slots[j] = jnp.where(take, s, slots[j])
            locals_[j] = jnp.where(take, their_local[s], locals_[j])
        count = count + here.astype(jnp.int32)
    q1s[...] = jnp.zeros_like(q1s)
    for b in range(BD):
        q1s[b, 0:GH, :] = q_ref[0, b]
    e1s[pl.ds(ALL, 2 * GH), :] = jnp.full((2 * GH, HD), -1e30, F32)
    v1s[pl.ds(ALL, 2 * GH), :] = jnp.zeros((2 * GH, HD), F32)
    for s in range(BD + MOST):
        rows = pl.ds(s * GH, GH)
        if s < BD:
            q = q_ref[1, s].astype(F32)
            step = kv_ref[1, s].astype(F32)
            parent = own_local[s]
        else:
            block = msg_ref[slots[s - BD]].astype(F32)
            q = block[0:GH]
            step = block[GH : GH + 2]
            parent = locals_[s - BD]
        pcol[rows, :] = jnp.full((GH, HD), parent, jnp.int32)
        q2s[rows, :] = q
        e1s[rows, :] = jnp.broadcast_to(
            jnp.sum(q * step[0:1], axis=1, keepdims=True) * scaling, (GH, HD)
        )
        v1s[rows, :] = jnp.broadcast_to(step[1:2], (GH, HD))
    q2 = q2s[...].astype(BF16)
    acc[...] = jnp.zeros_like(acc)
    places = lax.broadcasted_iota(jnp.int32, (1, CACHE), 1)
    def match(b):
        q = jnp.concatenate([q2, q1s[b]], axis=0)
        return q, lax.dot_general(
            q,
            cache_ref[b, 0 : PARTS // 2].reshape(CACHE, HD),
            (((1,), (1,)), ((), ())),
            preferred_element_type=F32,
        )

    def weigh(b, q, logits):
        bias = jnp.where(places < len_ref[mine + b], 0.0, -1e30)
        logits = logits * scaling + bias
        step = kv_ref[0, b].astype(F32)
        e0 = jnp.sum(q.astype(F32) * step[0:1], axis=1, keepdims=True) * scaling
        e1 = e1s[:, 0:1]
        peak = jnp.maximum(jnp.maximum(jnp.max(logits, axis=1, keepdims=True), e0), e1)
        p = jnp.exp2(logits - peak)
        p0 = jnp.exp2(e0 - peak)
        p1 = jnp.exp2(e1 - peak)
        inv = 1.0 / (jnp.sum(p, axis=1, keepdims=True) + p0 + p1)
        return p, p0, p1, inv, step

    def mix(b, p, p0, p1, inv, step):
        mixed = jnp.dot(
            (p * inv).astype(BF16),
            cache_ref[b, PARTS // 2 : PARTS].reshape(CACHE, HD),
            preferred_element_type=F32,
        )
        mixed = mixed + (p0 * inv).astype(BF16).astype(F32) * step[1:2]
        mixed = mixed + (p1 * inv).astype(BF16).astype(F32) * v1s[...]
        fscr[b * GH : (b + 1) * GH, :] = mixed[ALL : ALL + GH]
        acc[...] = jnp.where(pcol[...] == b, mixed[:ALL], acc[...])

    first = match(0)
    second = match(1)
    held = weigh(0, *first)
    for b in range(BD):
        third = match(b + 2) if b + 2 < BD else None
        ahead = weigh(b + 1, *second) if b + 1 < BD else None
        mix(b, *held)
        held, second = ahead, third
    rscr[...] = jnp.zeros_like(rscr)
    at = pl.multiple_of(half * BD, BD)
    their = pl.multiple_of((1 - half) * BD, BD)
    for h in range(GH):
        lanes = slice(h * HD, (h + 1) * HD)
        first_ref[:, lanes] = fscr[pl.ds(h, BD, stride=GH), :].astype(BF16)
        rscr[pl.ds(at, BD), lanes] = acc[pl.ds(h, BD, stride=GH), :].astype(BF16).astype(F32)
        crow[0:MOST, lanes] = acc[pl.ds(OWN + h, MOST, stride=GH), :].astype(BF16).astype(F32)
    for j in range(MOST):

        @pl.when(j < count)
        def _():
            rscr[pl.ds(their + slots[j], 1), :] = crow[j : j + 1, :]

    lane = lax.broadcasted_iota(jnp.int32, (BD, HD), 1)
    flags = jnp.zeros((BD, HD), F32)
    for s in range(BD):
        theirs_flag = msg_ref[s].astype(F32)[GH + 2 : GH + 3, :]
        flags = jnp.where(lane == their + s, theirs_flag, flags)
        flags = jnp.where(lane == at + s, fin_ref[s].astype(F32), flags)
    before = flags
    for k in range(4):
        moved = pltpu.roll(before, 1 << k, 1)
        before = before + jnp.where(lane >= 1 << k, moved, 0.0)
    rank = lax.broadcasted_iota(jnp.int32, (BD, HD), 0).astype(F32)
    pick = jnp.where((flags > 0.5) & (before - 1.0 == rank), 1.0, 0.0)
    packed = jnp.dot(
        pick[:, 0 : 2 * BD].astype(BF16), rscr[...].astype(BF16), preferred_element_type=F32
    )
    pick_ref[...] = pltpu.roll(pick, jnp.where(half == 1, HD - BD, 0), 1)
    own_ref[...] = rscr[pl.ds(at, BD), :].astype(BF16)
    rows_ref[...] = packed.astype(BF16)
    swap_ref[...] = jnp.concatenate([rscr[pl.ds(their, BD), :], packed], axis=0).astype(BF16)
    cross_local = locals_of(par_ref, mine, 1 - half)
    ranks, _, _ = needed(cross_local)
    for s in range(BD):
        slot = jnp.int32(-1)
        for b in range(BD):
            slot = jnp.where(cross_local[s] == b, ranks[b], slot)
        meta_ref[s : s + 1, :] = jnp.full((1, HD), slot, jnp.int32)
    for r in range(MOST):

        @pl.when(r < send_total)
        def _():
            late_copy(r).wait()

    for s in range(BD):

        @pl.when(own_local[s] >= 0)
        def _():
            pltpu.make_async_copy(cache_ref.at[0], newc_ref.at[s], outsem.at[s]).wait()


def place_kernel(first, meta_ref, recv_ref, pick_ref, *refs):
    token_ref, newc_ref, sems = refs[-3:]
    token_ref[...] = pick_ref[...]
    count = recv_ref.shape[0]
    copies = []
    for s in range(BD):
        rank = meta_ref[s : s + 1, :][0, 0]
        part = min(count, PARTS - first)
        copies.append(
            (rank == 0, recv_ref.at[pl.ds(0, part)], newc_ref.at[s, pl.ds(first, part)], sems.at[s])
        )
        if count > PARTS:
            at = jnp.clip(rank * PARTS - first, 0, count - PARTS)
            copies.append((rank > 0, recv_ref.at[pl.ds(at, PARTS)], newc_ref.at[s], sems.at[s]))
    for fits, source, target, sem in copies:

        @pl.when(fits)
        def _():
            pltpu.make_async_copy(source, target, sem).start()

    for fits, source, target, sem in copies:

        @pl.when(fits)
        def _():
            pltpu.make_async_copy(source, target, sem).wait()


def gate_kernel(*refs):
    del refs


def join_kernel(own_ref, rows_ref, swap_ref, *refs):
    second_ref, full_ref = refs
    second_ref[...] = own_ref[...] + swap_ref[0:BD, :]
    full_ref[...] = rows_ref[...] + swap_ref[BD : 2 * BD, :]


def hidden_kernel(own_ref, r1, r2, r3, w0, w1, w2, w3, out_ref):
    depth = w0.shape[0] - 16
    odd = lax.rem(lax.axis_index("dp"), 2) == 1
    near, far = r1[...].astype(F32), r2[...].astype(F32)
    rows = jnp.concatenate(
        [
            own_ref[...].astype(F32),
            jnp.where(odd, near, far),
            r3[...].astype(F32),
            jnp.where(odd, far, near),
        ],
        axis=0,
    )
    narrow = rows.astype(BF16)
    parts = [
        jnp.dot(narrow, w[0:depth, :], preferred_element_type=F32) for w in (w0, w1, w2, w3)
    ]
    squares = jnp.sum(rows * rows, axis=1, keepdims=True)
    parts.append(jnp.broadcast_to(squares, (rows.shape[0], HD)))
    for k in range(out_ref.shape[0]):
        for i, part in enumerate(parts):
            out_ref[k, :, i * HD : (i + 1) * HD] = part.astype(out_ref.dtype)


def score_kernel(hid_ref, w0, w1, w2, w3, out_ref):
    depth = w0.shape[0] - 16
    total = hid_ref[0].astype(F32)
    for k in range(1, hid_ref.shape[0]):
        total = total + hid_ref[k].astype(F32)
    factor = lax.rsqrt(total[:, 4 * HD : 4 * HD + 1] / D_GEN + 1e-05)
    sums = jnp.zeros((total.shape[0], 1), F32)
    for i, w in enumerate((w0, w1, w2, w3)):
        head = w[depth : depth + 16, :].astype(F32)[0:1, :]
        v = total[:, i * HD : (i + 1) * HD] * factor
        sums = sums + jnp.sum(v / (1.0 + jnp.exp(-v)) * head, axis=1, keepdims=True)
    wide = jnp.broadcast_to(sums, (total.shape[0], HD))
    pairs = out_ref.shape[0]
    mine = lax.rem(lax.axis_index("dp") // 2, pairs)
    for q in range(pairs):
        out_ref[lax.rem(mine + q, pairs)] = wide[q * BD : (q + 1) * BD]


def spread_kernel(own_ref, near_ref, far_ref, two_ref, three_ref):
    two_ref[...] = near_ref[...] + far_ref[...]
    three_ref[...] = own_ref[...] + two_ref[...]


def final_kernel(pick_ref, own_ref, two_ref, three_ref, out_ref):
    pair = lax.rem(lax.axis_index("dp") // 2, own_ref.shape[0])
    total = own_ref[pair] + two_ref[pair] + three_ref[pair]
    sums = jnp.sum(pick_ref[...] * total, axis=0, keepdims=True)
    for s in range(BD):
        out_ref[s] = sums[0, s]


def call(kernel, outs, ins, out_specs, scratch=(), aliases=None, cost=None, limit=60):
    return functools.partial(
        pl.pallas_call,
        kernel,
        out_shape=outs,
        in_specs=[spec(s) for s in ins],
        out_specs=[spec(s) for s in out_specs],
        scratch_shapes=list(scratch),
        input_output_aliases=aliases or {},
        compiler_params=pltpu.CompilerParams(vmem_limit_bytes=limit * 1024 * 1024),
        cost_estimate=pl.CostEstimate(flops=cost or 1000000, bytes_accessed=cost or 1000000, transcendentals=0),
    )()


def shape(dims, dtype):
    return jax.ShapeDtypeStruct(dims, dtype)


def swap(array):
    return lax.ppermute(array, "dp", [(i, i ^ 1) for i in range(lax.axis_size("dp"))])


def place(first, meta, recv, pick, newc):
    return call(
        functools.partial(place_kernel, first),
        [shape(pick.shape, F32), shape(newc.shape, BF16)],
        [VM, VM, VM, HB],
        [VM, HB],
        [pltpu.SemaphoreType.DMA((BD,))],
        aliases={3: 1},
        limit=16,
    )(meta, recv, pick, newc)


def away(array, nz, k):
    nd = lax.axis_size("dp")
    pairs = []
    for d in range(nd):
        z = d % nz
        pairs.append((d, d - z + (z - k if z % 2 == 0 else z + k) % nz))
    return lax.ppermute(array, "dp", pairs)


EARLY = 2


def per_device(nx, nz, cache_kv, lengths, step_kv, queries, parents, finished, reward_in, reward_head):
    ndp = nx * nz
    nt = lax.axis_size("tensor")
    cache = cache_kv.reshape(BD, PARTS, 2 * CACHE // PARTS, HD)
    kv = step_kv.reshape(2, BD, 2, HD)
    depth = reward_in.shape[0]
    part_a = shape((EARLY,) + cache.shape[2:], BF16)
    part_b = shape((MOST * PARTS - EARLY,) + cache.shape[2:], BF16)
    msg, early, wext = call(
        pack_kernel,
        [shape((BD, 16, HD), BF16), part_a, shape((depth + 16, HD), BF16)],
        [SM, SM, HB, HB, VM, VM, VM],
        [VM, VM, VM],
        [pltpu.SemaphoreType.DMA, pltpu.SemaphoreType.DMA],
        limit=57,
        cost=1000000,
    )(parents, finished, cache, reward_in, reward_head.reshape(1, HD), queries, kv)
    recv_msg = swap(msg)
    (early,) = call(
        gate_kernel, [part_a], [pl.ANY, pl.ANY], [pl.ANY], aliases={0: 0}, limit=16, cost=1000
    )(early, recv_msg)
    recv_early = swap(early)
    near_w, far_w = (
        lax.ppermute(wext, "dp", [(i, (i + nz * k) % ndp) for i in range(ndp)]) for k in (1, nx - 1)
    )
    others = [near_w, lax.ppermute(near_w, "dp", [(i, (i + nz) % ndp) for i in range(ndp)]), far_w]
    first_out, own_out, to_swap, rows, meta, pick, late, newc = call(
        attend_kernel,
        [
            shape((BD, GH * HD), BF16),
            shape((BD, GH * HD), BF16),
            shape((2 * BD, GH * HD), BF16),
            shape((BD, GH * HD), BF16),
            shape((BD, HD), jnp.int32),
            shape((BD, HD), F32),
            part_b,
            shape(cache.shape, BF16),
        ],
        [SM, SM, SM, VM, VM, VM, VM],
        [VM] * 7 + [HB],
        [
            VM((ALL, HD), F32),
            VM((BD, 2 * GH, HD), BF16),
            VM((ROWS, HD), F32),
            VM((ROWS, HD), F32),
            VM((ALL, HD), jnp.int32),
            VM((OWN, HD), F32),
            VM((ALL, HD), F32),
            VM((2 * BD, GH * HD), F32),
            VM((BD, GH * HD), F32),
            pltpu.SemaphoreType.DMA((BD,)),
            pltpu.SemaphoreType.DMA((MOST,)),
        ],
        cost=20000000,
        limit=32,
    )(parents, lengths, finished, cache, queries, kv, recv_msg)
    recv_swap = swap(to_swap)
    (late,) = call(
        gate_kernel, [part_b], [pl.ANY] * 5, [pl.ANY], aliases={0: 0}, limit=16, cost=1000
    )(late, recv_swap, recv_early, others[0], others[2])
    second_out, rows = call(
        join_kernel,
        [shape(own_out.shape, BF16), shape(rows.shape, BF16)],
        [VM] * 3,
        [VM, VM],
        limit=16,
    )(own_out, rows, recv_swap)
    recv_late = swap(late)
    (partial,) = call(
        hidden_kernel, [shape((nt, nz // 2 * BD, 5 * HD), BF16)], [VM] * 8, [VM], limit=16
    )(rows, *[away(rows, nz, k) for k in (1, 2, 3)], wext, *others)
    partials = lax.all_to_all(partial, "tensor", 0, 0, tiled=True)
    (sums,) = call(
        score_kernel, [shape((nz // 2, BD, HD), F32)], [VM] * 5, [VM], limit=16
    )(partials, wext, *others)
    two, three = call(
        spread_kernel, [shape(sums.shape, F32)] * 2, [VM] * 3, [VM] * 2, limit=16
    )(sums, away(sums, nz, 1), away(sums, nz, 2))
    pick, newc = place(0, meta, recv_early, pick, newc)
    pick, newc = place(EARLY, meta, recv_late, pick, newc)
    (scores,) = call(
        final_kernel, [shape((BD,), F32)], [VM] * 4, [SM], limit=16
    )(pick, three, away(two, nz, 2), away(three, nz, 3))
    return (first_out, second_out, scores, newc.reshape(cache_kv.shape))


def solution(mesh):
    ndp = mesh.shape["dp"]
    nx = 4
    return jax.shard_map(
        functools.partial(per_device, nx, ndp // nx),
        mesh=mesh,
        in_specs=(
            P("dp", None, None, "tensor", None),
            P(),
            P(None, "dp", None, "tensor", None),
            P(None, "dp", "tensor", None),
            P(),
            P("dp"),
            P("tensor", "dp"),
            P("dp"),
        ),
        out_specs=(
            P("dp", "tensor"),
            P("dp", "tensor"),
            P("dp"),
            P("dp", None, None, "tensor", None),
        ),
        check_vma=False,
    )
```
